32 devices in a mesh: fsdp: 2 (over x), context: 16 (over z, y, core).
Axes of the slice: x: 2, y: 2, z: 4, core: 2. Of those that a mesh axis runs over, the one named last changes fastest.
Arguments:
- tokens: bfloat16 [2, 2048, 1600], P('fsdp', 'context'), may hold values from -6 to 6
- cotangent: bfloat16 [2, 2048, 1600], P('fsdp', 'context'), may hold values from -6 to 6
- block_order: int32 [32], replicated, may hold values from 0 to 31, each once
- ln1_gain: bfloat16 [1600], P('fsdp'), may hold values from 0.5 to 1.5
- ln1_bias: bfloat16 [1600], P('fsdp'), may hold values from -3 to 3
- w_qkv: bfloat16 [1600, 4800], P('context', 'fsdp'), may hold values from -5.05 to 5.05
- qv_bias: bfloat16 [1600, 2], P('fsdp'), may hold values from -0.29882812 to 0.29882812
- w_out: bfloat16 [1600, 1600], P('context', 'fsdp'), may hold values from -0.875 to 0.875
- out_bias: bfloat16 [1600], P('fsdp'), may hold values from -3 to 3
- ln2_gain: bfloat16 [1600], P('fsdp'), may hold values from 0.5 to 1.5
- ln2_bias: bfloat16 [1600], P('fsdp'), may hold values from -3 to 3
- w_fc: bfloat16 [1600, 6400], P('context', 'fsdp'), may hold values from -0.15625 to 0.15625
- fc_bias: bfloat16 [6400], P('fsdp'), may hold values from -3 to 3
- w_proj: bfloat16 [6400, 1600], P('context', 'fsdp'), may hold values from -0.078125 to 0.078125
- proj_bias: bfloat16 [1600], P('fsdp'), may hold values from -3 to 3
Outputs:
- out: bfloat16 [2, 2048, 1600], P('fsdp', 'context')
- d_tokens: bfloat16 [2, 2048, 1600], P('fsdp', 'context')
- g_ln1_gain: float32 [1600], P('fsdp')
- g_ln1_bias: float32 [1600], P('fsdp')
- g_w_qkv: float32 [1600, 4800], P('context', 'fsdp')
- g_qv_bias: float32 [1600, 2], P('fsdp')
- g_w_out: float32 [1600, 1600], P('context', 'fsdp')
- g_out_bias: float32 [1600], P('fsdp')
- g_ln2_gain: float32 [1600], P('fsdp')
- g_ln2_bias: float32 [1600], P('fsdp')
- g_w_fc: float32 [1600, 6400], P('context', 'fsdp')
- g_fc_bias: float32 [6400], P('fsdp')
- g_w_proj: float32 [6400, 1600], P('context', 'fsdp')
- g_proj_bias: float32 [1600], P('fsdp')
The draws below stay inside these ranges and needn't reach their ends.
Inputs may be any that keep to these rules, and one draw needn't show every extreme that they name: block_order names each of the 32 blocks of positions once; rows s * 64 to s * 64 + 63 of a sequence hold positions block_order[s] * 64 onward, in order.
All inputs are finite; a program needn't handle non-finite values.
Results may differ from the reference program's by a relative error of at most 0.025.
Values may be sent and summed in bfloat16 or wider, within the bound.
No kernel may reach another device: no remote copies, remote signals or barrier semaphores. Data moves between devices by JAX's collectives and lax.ppermute only.
A program may use at most 576 MiB of HBM per device.

```python
import math
import jax
import jax.numpy as jnp
from jax import lax

HEADS = 25
HEAD_DIM = 64
D = 1600
FF = 6400
BLK = 64
SEQ_LEN = 2048
SEQS = 2
TOKENS = 4096
N_CONTEXT = 16


def draw_w_qkv(key, part):
    width = HEADS * HEAD_DIM
    first_key = jax.random.fold_in(jax.random.fold_in(key, 7), 0)
    drawn = jnp.clip(jax.random.normal(first_key, (width, 3 * width), jnp.float32), -5.0, 5.0) * width ** (-0.5)
    return drawn.astype(jnp.bfloat16)


def shard_levels(key, extent, cuts, least, largest):
    gain = 1.0
    for axis_at, shards_of in cuts:
        steps = jax.random.uniform(jax.random.fold_in(jax.random.fold_in(key, 6), axis_at), (shards_of,), jnp.float32, least / len(cuts), largest / len(cuts))
        gain = gain * jnp.repeat(jnp.exp(steps), extent[axis_at] // shards_of).reshape((-1,) + (1,) * (len(extent) - 1 - axis_at))
    return gain


def gaussian(stream_key, extent, deviation, bound, pieces=(), kind=jnp.bfloat16):
    values = deviation * jax.random.normal(stream_key, extent, jnp.float32)
    if pieces:
        values = values * shard_levels(stream_key, extent, pieces, -0.22, 0.18)
    return jnp.clip(values, -bound, bound).astype(kind)


def setup_inputs(seed: int = 0) -> dict:
    key_of = jax.random.split(jax.random.key(seed), 16)
    return {
        "tokens": gaussian(key_of[0], (SEQS, SEQ_LEN, D), 1.0, 6.0, ((0, 2), (1, 16))),
        "cotangent": gaussian(key_of[1], (SEQS, SEQ_LEN, D), 1.0, 6.0, ((0, 2), (1, 16))),
        "block_order": jax.random.permutation(key_of[2], 2 * N_CONTEXT).astype(jnp.int32),
        "ln1_gain": jnp.clip(1.0 + 0.1 * jax.random.normal(key_of[3], (D,), jnp.float32), 0.5, 1.5).astype(jnp.bfloat16),
        "ln1_bias": gaussian(key_of[4], (D,), 0.5, 3.0, ((0, 2),)),
        "w_qkv": draw_w_qkv(jax.random.fold_in(key_of[15], 71), 0),
        "qv_bias": gaussian(key_of[6], (D, 2), 0.05, 0.29882812, ((0, 2),)),
        "w_out": gaussian(key_of[7], (D, D), (max(1, 64 * D // SEQ_LEN)) ** -0.5, 0.875, ((0, 16), (1, 2))),
        "out_bias": gaussian(key_of[8], (D,), 0.5, 3.0, ((0, 2),)),
        "ln2_gain": jnp.clip(1.0 + 0.1 * jax.random.normal(key_of[9], (D,), jnp.float32), 0.5, 1.5).astype(jnp.bfloat16),
        "ln2_bias": gaussian(key_of[10], (D,), 0.5, 3.0, ((0, 2),)),
        "w_fc": gaussian(key_of[11], (D, FF), D ** -0.5, 0.15625, ((0, 16), (1, 2))),
        "fc_bias": gaussian(key_of[12], (FF,), 0.5, 3.0, ((0, 2),)),
        "w_proj": gaussian(key_of[13], (FF, D), FF ** -0.5, 0.078125, ((0, 16), (1, 2))),
        "proj_bias": gaussian(key_of[14], (D,), 0.5, 3.0, ((0, 2),)),
    }


EPSILON = 1e-05
GELU_ROOT = math.sqrt(2.0 / math.pi)
GELU_CUBIC = 0.044715
NEG_LARGE = -1e+30

def normalize(values, gain_vec, bias_vec):
    centred = values - lax.optimization_barrier(jnp.mean(values, axis=-1, keepdims=True))
    inv_std = lax.rsqrt(lax.optimization_barrier(jnp.mean(centred * centred, axis=-1, keepdims=True)) + EPSILON)
    normed = centred * inv_std
    return (normed * gain_vec.astype(jnp.float32) + bias_vec.astype(jnp.float32), normed, inv_std)

def norm_back(upstream, normed, inv_std, gain_vec):
    scaled = upstream * gain_vec.astype(jnp.float32)
    return inv_std * (scaled - lax.optimization_barrier(jnp.mean(scaled, axis=-1, keepdims=True)) - normed * lax.optimization_barrier(jnp.mean(scaled * normed, axis=-1, keepdims=True)))

def gelu_pair(pre_act):
    inner = GELU_ROOT * (pre_act + GELU_CUBIC * pre_act * pre_act * pre_act)
    tangent = jnp.tanh(inner)
    act_value = 0.5 * pre_act * (1.0 + tangent)
    act_slope = 0.5 * (1.0 + tangent) + 0.5 * pre_act * (1.0 - tangent * tangent) * GELU_ROOT * (1.0 + 3.0 * GELU_CUBIC * pre_act * pre_act)
    return (act_value, act_slope)

def positions_of(block_order, block_len):
    offsets = jnp.arange(block_len, dtype=jnp.int32)
    return (block_order.astype(jnp.int32)[:, None] * block_len + offsets[None, :]).reshape(-1)

def forward_attention(queries, keys, values, key_pos):
    length = queries.shape[0]
    qblock = math.gcd(length, 256)
    block_count = length // qblock
    score_scale = HEAD_DIM ** (-0.5)
    q_heads = queries.astype(jnp.float32).reshape(block_count, qblock, HEADS, HEAD_DIM)
    k_heads = keys.astype(jnp.float32).reshape(length, HEADS, HEAD_DIM)
    v_heads = values.astype(jnp.float32).reshape(length, HEADS, HEAD_DIM)
    q_pos = key_pos.reshape(block_count, qblock)

    def one_block(inputs):
        query_rows, query_pos = inputs
        scores = jnp.einsum('qhd,khd->hqk', query_rows, k_heads) * score_scale
        allowed = (query_pos[:, None] >= key_pos[None, :])[None]
        maxima = lax.optimization_barrier(jnp.max(jnp.where(allowed, scores, NEG_LARGE), axis=-1))
        totals = lax.optimization_barrier(jnp.sum(jnp.where(allowed, jnp.exp(scores - maxima[..., None]), 0.0), axis=-1))
        log_norm = maxima + jnp.log(totals)
        prob_rows = jnp.where(allowed, jnp.exp(scores - log_norm[..., None]), 0.0)
        prob_half = lax.optimization_barrier(prob_rows.astype(jnp.bfloat16)).astype(jnp.float32)
        mixed = jnp.einsum('hqk,khd->qhd', prob_half, v_heads)
        return (mixed.reshape(qblock, HEADS * HEAD_DIM).astype(jnp.bfloat16), log_norm)
    outputs, log_norms = lax.map(one_block, (q_heads, q_pos))
    return (outputs.reshape(length, HEADS * HEAD_DIM), log_norms)

def backward_attention(queries, keys, values, key_pos, log_norms, grad_out, attn_out):
    length = queries.shape[0]
    qblock = math.gcd(length, 256)
    block_count = length // qblock
    score_scale = HEAD_DIM ** (-0.5)
    q_heads = queries.astype(jnp.float32).reshape(block_count, qblock, HEADS, HEAD_DIM)
    g_heads = grad_out.astype(jnp.float32).reshape(block_count, qblock, HEADS, HEAD_DIM)
    o_heads = attn_out.astype(jnp.float32).reshape(block_count, qblock, HEADS, HEAD_DIM)
    k_heads = keys.astype(jnp.float32).reshape(length, HEADS, HEAD_DIM)
    v_heads = values.astype(jnp.float32).reshape(length, HEADS, HEAD_DIM)
    q_pos = key_pos.reshape(block_count, qblock)

    def one_block(carry, inputs):
        key_grad, value_grad = carry
        query_rows, query_pos, log_norm, grad_rows, out_rows = inputs
        scores = jnp.einsum('qhd,khd->hqk', query_rows, k_heads) * score_scale
        allowed = (query_pos[:, None] >= key_pos[None, :])[None]
        prob_full = jnp.where(allowed, jnp.exp(scores - log_norm[..., None]), 0.0)
        prob_half = lax.optimization_barrier(prob_full.astype(jnp.bfloat16)).astype(jnp.float32)
        row_dot = lax.optimization_barrier(jnp.sum(grad_rows * out_rows, axis=-1)).T
        value_grad = value_grad + jnp.einsum('hqk,qhd->khd', prob_half, grad_rows)
        dprob = jnp.einsum('qhd,khd->hqk', grad_rows, v_heads)
        dscore = score_scale * prob_full * (dprob - row_dot[..., None])
        dscore = lax.optimization_barrier(dscore.astype(jnp.bfloat16)).astype(jnp.float32)
        query_grad = jnp.einsum('hqk,khd->qhd', dscore, k_heads)
        key_grad = key_grad + jnp.einsum('hqk,qhd->khd', dscore, query_rows)
        return ((key_grad, value_grad), query_grad.reshape(qblock, HEADS * HEAD_DIM))
    zeros = jnp.zeros((length, HEADS, HEAD_DIM), jnp.float32)
    (key_grad, value_grad), query_grad = lax.scan(one_block, (zeros, zeros), (q_heads, q_pos, log_norms, g_heads, o_heads))
    width = HEADS * HEAD_DIM
    return (query_grad.reshape(length, width), key_grad.reshape(length, width), value_grad.reshape(length, width))

def one_sequence(inputs, cot_rows, key_pos, ln1_gain, ln1_bias, w_qkv, qv_bias, w_out, out_bias, ln2_gain, ln2_bias, w_fc, fc_bias, w_proj, proj_bias):
    width = HEADS * HEAD_DIM
    xs = inputs.astype(jnp.float32)
    h_one, normed_one, inv_one = normalize(xs, ln1_gain, ln1_bias)
    h_one = h_one.astype(jnp.bfloat16)
    qkv = jnp.dot(h_one, w_qkv, preferred_element_type=jnp.float32)
    queries = (qkv[:, :width] + qv_bias[:, 0].astype(jnp.float32)).astype(jnp.bfloat16)
    keys = qkv[:, width:2 * width].astype(jnp.bfloat16)
    values = (qkv[:, 2 * width:] + qv_bias[:, 1].astype(jnp.float32)).astype(jnp.bfloat16)
    attn_out, log_norms = forward_attention(queries, keys, values, key_pos)
    resid_one = xs + jnp.dot(attn_out, w_out, preferred_element_type=jnp.float32) + out_bias.astype(jnp.float32)
    h_two, normed_two, inv_two = normalize(resid_one, ln2_gain, ln2_bias)
    h_two = h_two.astype(jnp.bfloat16)
    pre_act = jnp.dot(h_two, w_fc, preferred_element_type=jnp.float32) + fc_bias.astype(jnp.float32)
    act_value, act_slope = gelu_pair(pre_act)
    act_half = act_value.astype(jnp.bfloat16)
    result = resid_one + jnp.dot(act_half, w_proj, preferred_element_type=jnp.float32) + proj_bias.astype(jnp.float32)
    grad_y = cot_rows.astype(jnp.float32)
    g_w_proj = jnp.dot(act_half.T, cot_rows, preferred_element_type=jnp.float32)
    g_proj_bias = lax.optimization_barrier(jnp.sum(grad_y, axis=0))
    grad_pre = jnp.dot(cot_rows, w_proj.T, preferred_element_type=jnp.float32) * act_slope
    g_fc_bias = lax.optimization_barrier(jnp.sum(grad_pre, axis=0))
    grad_pre16 = grad_pre.astype(jnp.bfloat16)
    g_w_fc = jnp.dot(h_two.T, grad_pre16, preferred_element_type=jnp.float32)
    grad_h2 = jnp.dot(grad_pre16, w_fc.T, preferred_element_type=jnp.float32)
    g_ln2_gain = lax.optimization_barrier(jnp.sum(grad_h2 * normed_two, axis=0))
    g_ln2_bias = lax.optimization_barrier(jnp.sum(grad_h2, axis=0))
    grad_r1 = grad_y + norm_back(grad_h2, normed_two, inv_two, ln2_gain)
    g_out_bias = lax.optimization_barrier(jnp.sum(grad_r1, axis=0))
    grad_r16 = grad_r1.astype(jnp.bfloat16)
    g_w_out = jnp.dot(attn_out.T, grad_r16, preferred_element_type=jnp.float32)
    grad_o16 = jnp.dot(grad_r16, w_out.T, preferred_element_type=jnp.float32).astype(jnp.bfloat16)
    grad_q, grad_k, grad_v = backward_attention(queries, keys, values, key_pos, log_norms, grad_o16, attn_out)
    g_qv_bias = jnp.stack([lax.optimization_barrier(jnp.sum(grad_q, axis=0)), lax.optimization_barrier(jnp.sum(grad_v, axis=0))], axis=1)
    grad_qkv16 = jnp.concatenate([grad_q, grad_k, grad_v], axis=1).astype(jnp.bfloat16)
    g_w_qkv = jnp.dot(h_one.T, grad_qkv16, preferred_element_type=jnp.float32)
    grad_h1 = jnp.dot(grad_qkv16, w_qkv.T, preferred_element_type=jnp.float32)
    g_ln1_gain = lax.optimization_barrier(jnp.sum(grad_h1 * normed_one, axis=0))
    g_ln1_bias = lax.optimization_barrier(jnp.sum(grad_h1, axis=0))
    grad_x = (grad_r1 + norm_back(grad_h1, normed_one, inv_one, ln1_gain)).astype(jnp.bfloat16)
    grads = (g_ln1_gain, g_ln1_bias, g_w_qkv, g_qv_bias, g_w_out, g_out_bias, g_ln2_gain, g_ln2_bias, g_w_fc, g_fc_bias, g_w_proj, g_proj_bias)
    return (result.astype(jnp.bfloat16), grad_x, grads)

def reference(tokens, cotangent, block_order, ln1_gain, ln1_bias, w_qkv, qv_bias, w_out, out_bias, ln2_gain, ln2_bias, w_fc, fc_bias, w_proj, proj_bias):
    grad_scale = 1.0 / math.sqrt(TOKENS)
    key_pos = positions_of(block_order, BLK)
    results = []
    input_grads = []
    totals = None
    for sequence in range(SEQS):
        result, grad_x, grads = one_sequence(tokens[sequence], cotangent[sequence], key_pos, ln1_gain, ln1_bias, w_qkv, qv_bias, w_out, out_bias, ln2_gain, ln2_bias, w_fc, fc_bias, w_proj, proj_bias)
        results.append(result)
        input_grads.append(grad_x)
        if totals is None:
            totals = grads
        else:
            totals = jax.tree.map(lambda left, right: left + right, totals, grads)
    scaled = jax.tree.map(lambda entry: entry * grad_scale, totals)
    return (jnp.stack(results), jnp.stack(input_grads), scaled[0], scaled[1], scaled[2], scaled[3], scaled[4], scaled[5], scaled[6], scaled[7], scaled[8], scaled[9], scaled[10], scaled[11])
```

```python
import functools
import math

import jax
import jax.numpy as jnp
from jax import lax
from jax.experimental import pallas as pl
from jax.experimental.pallas import tpu as pltpu
from jax.sharding import PartitionSpec as P

HEADS = 25
HEAD_DIM = 64
SLOT = 2 * HEAD_DIM

EPSILON = 1e-05
GELU_ROOT = math.sqrt(2.0 / math.pi)
GELU_CUBIC = 0.044715
NEG_LARGE = -1e30
SCALE = HEAD_DIM ** (-0.5)
VMEM_LIMIT = 56 * 1024 * 1024
F32 = jnp.float32
BF16 = jnp.bfloat16


def norm_stats(values):
    centred = values - jnp.mean(values, axis=-1, keepdims=True)
    inv_std = lax.rsqrt(jnp.mean(centred * centred, axis=-1, keepdims=True) + EPSILON)
    return centred * inv_std, inv_std


def norm_back(upstream, normed, inv_std, gain_vec):
    scaled = upstream * gain_vec
    return inv_std * (
        scaled
        - jnp.mean(scaled, axis=-1, keepdims=True)
        - normed * jnp.mean(scaled * normed, axis=-1, keepdims=True)
    )


def gelu_pair(pre_act):
    inner = GELU_ROOT * (pre_act + GELU_CUBIC * pre_act * pre_act * pre_act)
    tangent = jnp.tanh(inner)
    act_value = 0.5 * pre_act * (1.0 + tangent)
    act_slope = 0.5 * (1.0 + tangent) + 0.5 * pre_act * (1.0 - tangent * tangent) * GELU_ROOT * (
        1.0 + 3.0 * GELU_CUBIC * pre_act * pre_act
    )
    return (act_value, act_slope)


class Ring:
    def __init__(self, count):
        chips = count // 2
        self.count, self.size = count, chips
        self.mine = lax.axis_index("context")
        self.core = self.mine % 2
        chip = self.mine // 2
        if chips == 8:
            order = [0, 2, 4, 6, 7, 5, 3, 1]
            self.place = jnp.where(chip % 2 == 0, chip // 2, (15 - chip) // 2)
        else:
            order = list(range(chips))
            self.place = chip
        self.right = []
        self.left = []
        for i in range(chips):
            for core in range(2):
                here = 2 * order[i] + core
                self.right.append((here, 2 * order[(i + 1) % chips] + core))
                self.left.append((here, 2 * order[(i - 1) % chips] + core))
        self.swap = [(i, i ^ 1) for i in range(count)]

    def device(self, offset, other=0):
        at = (self.place + (offset % self.size)) % self.size
        chip = jnp.where(at < 4, 2 * at, 15 - 2 * at) if self.size == 8 else at
        return 2 * chip + (self.core ^ other)

    def send(self, value, links):
        return lax.ppermute(value, "context", links)

    def gather(self, block, place):
        far = self.size // 2
        to_right = to_left = block
        place(self.device(0), block, 0)
        place(self.device(0, 1), self.send(block, self.swap), 0)
        for step in range(1, far + 1):
            at_left = 0
            if step == far:
                to_right, to_left, at_left = to_right[:1], to_left[1:], 1
            to_right = self.send(to_right, self.right)
            to_left = self.send(to_left, self.left)
            place(self.device(-step), to_right, 0)
            place(self.device(step), to_left, at_left)
            place(self.device(-step, 1), self.send(to_right, self.swap), 0)
            place(self.device(step, 1), self.send(to_left, self.swap), at_left)

    def scatter(self, take):
        far = self.size // 2

        def term(offset):
            return add_half(take(self.device(offset)), self.send(take(self.device(offset, 1)), self.swap))

        last = term(far)
        to_right = self.send(last[:1], self.right)
        to_left = self.send(last[1:], self.left)
        for step in range(far - 1, 0, -1):
            right_term, left_term = term(step), term(-step)
            if step == far - 1:
                right_term = jnp.concatenate([add_half(right_term[:1], to_right), right_term[1:]], 0)
                left_term = jnp.concatenate([left_term[:1], add_half(left_term[1:], to_left)], 0)
            else:
                right_term, left_term = add_half(right_term, to_right), add_half(left_term, to_left)
            to_right = self.send(right_term, self.right)
            to_left = self.send(left_term, self.left)
        return term(0).astype(F32) + to_right.astype(F32) + to_left.astype(F32)


def add_half(first, second):
    return (first.astype(F32) + second.astype(F32)).astype(first.dtype)


def cross(value):
    return lax.ppermute(value, "fsdp", [(0, 1), (1, 0)])


def pair_halves(own, side):
    got = cross(own)
    return jnp.where(side == 0, own, got), jnp.where(side == 0, got, own)


def pair_sum(left, right, side):
    got = cross(jnp.where(side == 0, right, left).astype(BF16))
    return jnp.where(side == 0, left, right).astype(F32) + got.astype(F32)


def sum_everywhere(value, count):
    step = 1
    while step < count:
        value = value + lax.ppermute(value, "context", [(i, i ^ step) for i in range(count)])
        step *= 2
    return value + cross(value)


def dot_nt(first, second):
    return lax.dot_general(first, second, (((1,), (1,)), ((), ())), preferred_element_type=F32)


def dot_nn(first, second):
    return lax.dot_general(first, second, (((1,), (0,)), ((), ())), preferred_element_type=F32)


def head_masks(scale):
    lane = lax.broadcasted_iota(jnp.int32, (1, SLOT), 1)
    return [jnp.where(lane < HEAD_DIM, scale, 0.0), jnp.where(lane < HEAD_DIM, 0.0, scale)]


def flipped(value):
    return value.astype(F32).T


def causal(tile):
    keys = lax.broadcasted_iota(jnp.int32, (tile, tile), 0)
    queries = lax.broadcasted_iota(jnp.int32, (tile, tile), 1)
    return keys <= queries


def forward_kernel(order, q_ref, k_ref, v_ref, o_ref, lse_ref, qs, ks, vs, vt, os, *, blk, tile):
    seq = q_ref.shape[0]
    tiles = seq // tile
    masks = head_masks(SCALE)

    def span(index, size):
        return pl.ds(pl.multiple_of(index * size, size), size)

    def sort_in(s, carry):
        here, there = span(s, blk), span(order[s], blk)
        block = q_ref[here, :].astype(F32)
        for head in range(2):
            qs[head, there, :] = (block * masks[head]).astype(BF16)
        ks[there, :] = k_ref[here, :]
        vs[there, :] = v_ref[here, :]
        return carry

    lax.fori_loop(0, seq // blk, sort_in, 0)

    def turn(t, carry):
        vt[t] = flipped(vs[span(t, tile), :]).astype(BF16)
        return carry

    lax.fori_loop(0, tiles, turn, 0)
    visible = causal(tile)

    def query_tile(i, carry):
        def key_tile(j, state, diagonal):
            fresh = []
            for head in range(2):
                top, total, accum = state[3 * head : 3 * head + 3]
                scores = dot_nt(ks[span(j, tile), :], qs[head, span(i, tile), :])
                if diagonal:
                    scores = jnp.where(visible, scores, NEG_LARGE)
                new_top = jnp.maximum(top, jnp.max(scores, axis=0, keepdims=True))
                terms = jnp.exp(scores - new_top)
                decay = jnp.exp(top - new_top)
                total = total * decay + jnp.sum(terms, axis=0, keepdims=True)
                values = vt[j, head * HEAD_DIM : (head + 1) * HEAD_DIM, :]
                accum = accum * decay + dot_nn(values, terms.astype(BF16))
                fresh += [new_top, total, accum]
            return tuple(fresh)

        start = (
            jnp.full((1, tile), NEG_LARGE, F32),
            jnp.zeros((1, tile), F32),
            jnp.zeros((HEAD_DIM, tile), F32),
        )
        state = lax.fori_loop(0, i, lambda j, state: key_tile(j, state, False), start + start)
        state = key_tile(i, state, True)
        mixed = jnp.concatenate([state[2] / state[1], state[5] / state[4]], axis=0)
        os[span(i, tile), :] = mixed.T.astype(BF16)
        for head in range(2):
            lse_ref[i, head : head + 1, :] = state[3 * head] + jnp.log(state[3 * head + 1])
        return carry

    lax.fori_loop(0, tiles, query_tile, 0)

    def sort_out(s, carry):
        o_ref[span(s, blk), :] = os[span(order[s], blk), :]
        return carry

    lax.fori_loop(0, seq // blk, sort_out, 0)


def backward_kernel(
    order, q_ref, k_ref, v_ref, g_ref, o_ref, lse_ref, d_ref, sum_ref, qs, ks, vs, gs, ps, kt, dqt, drow, dk, dv, dsort, *, blk, tile
):
    seq = q_ref.shape[0]
    tiles = seq // tile
    q_masks, g_masks = head_masks(SCALE), head_masks(1.0)

    def span(index, size):
        return pl.ds(pl.multiple_of(index * size, size), size)

    def sort_in(s, carry):
        here, there = span(s, blk), span(order[s], blk)
        q_block, g_block = q_ref[here, :].astype(F32), g_ref[here, :].astype(F32)
        for head in range(2):
            qs[head, there, :] = (q_block * q_masks[head]).astype(BF16)
            gs[head, there, :] = (g_block * g_masks[head]).astype(BF16)
        ks[there, :] = k_ref[here, :]
        vs[there, :] = v_ref[here, :]
        ps[there, :] = g_block * o_ref[here, :].astype(F32)
        return carry

    lax.fori_loop(0, seq // blk, sort_in, 0)

    def turn(t, carry):
        kt[t] = flipped(ks[span(t, tile), :]).astype(BF16)
        products = ps[span(t, tile), :].T
        for head in range(2):
            drow[t, head : head + 1, :] = jnp.sum(
                products[head * HEAD_DIM : (head + 1) * HEAD_DIM], axis=0, keepdims=True
            )
        dqt[t] = jnp.zeros((SLOT, tile), F32)
        return carry

    lax.fori_loop(0, tiles, turn, 0)
    visible = causal(tile)
    sum_ref[...] = jnp.zeros(sum_ref.shape, F32)

    def key_tile(j, carry):
        dk[...] = jnp.zeros(dk.shape, F32)
        dv[...] = jnp.zeros(dv.shape, F32)

        def query_tile(i, diagonal):
            key_add, value_add = [], []
            for head in range(2):
                scores = dot_nt(ks[span(j, tile), :], qs[head, span(i, tile), :])
                terms = jnp.exp(scores - lse_ref[i, head : head + 1, :])
                if diagonal:
                    terms = jnp.where(visible, terms, 0.0)
                slopes = dot_nt(vs[span(j, tile), :], gs[head, span(i, tile), :])
                slopes = (terms * (slopes - drow[i, head : head + 1, :])).astype(BF16)
                value_add.append(dot_nn(terms.astype(BF16), gs[head, span(i, tile), :]))
                key_add.append(dot_nn(slopes, qs[head, span(i, tile), :]))
                rows = slice(head * HEAD_DIM, (head + 1) * HEAD_DIM)
                dqt[i, rows, :] += dot_nn(kt[j, rows, :], slopes)
            dk[...] += key_add[0] + key_add[1]
            dv[...] += value_add[0] + value_add[1]

        query_tile(j, True)

        def later(i, carry):
            query_tile(i, False)
            return carry

        lax.fori_loop(j + 1, tiles, later, 0)
        dsort[1, span(j, tile), :] = dk[...].astype(BF16)
        dsort[2, span(j, tile), :] = dv[...].astype(BF16)
        sum_ref[1:2, :] += jnp.sum(dv[...], axis=0, keepdims=True)
        return carry

    lax.fori_loop(0, tiles, key_tile, 0)

    def finish(t, carry):
        query_grad = dqt[t].T * SCALE
        dsort[0, span(t, tile), :] = query_grad.astype(BF16)
        sum_ref[0:1, :] += jnp.sum(query_grad, axis=0, keepdims=True)
        return carry

    lax.fori_loop(0, tiles, finish, 0)

    def sort_out(s, carry):
        for part in range(3):
            d_ref[span(s, blk), part * SLOT : (part + 1) * SLOT] = dsort[part, span(order[s], blk), :]
        return carry

    lax.fori_loop(0, seq // blk, sort_out, 0)


def tile_of(seq):
    return math.gcd(seq, 512)


VMEM_SPEC = pl.BlockSpec(memory_space=pltpu.VMEM)
SMEM_SPEC = pl.BlockSpec(memory_space=pltpu.SMEM)


def attend_forward(order, queries, keys, values, blk):
    seq = queries.shape[0]
    tile = tile_of(seq)
    return pl.pallas_call(
        functools.partial(forward_kernel, blk=blk, tile=tile),
        out_shape=(
            jax.ShapeDtypeStruct((seq, SLOT), BF16),
            jax.ShapeDtypeStruct((seq // tile, 8, tile), F32),
        ),
        in_specs=[SMEM_SPEC] + [VMEM_SPEC] * 3,
        out_specs=(VMEM_SPEC, VMEM_SPEC),
        scratch_shapes=[
            pltpu.VMEM((2, seq, SLOT), BF16),
            pltpu.VMEM((seq, SLOT), BF16),
            pltpu.VMEM((seq, SLOT), BF16),
            pltpu.VMEM((seq // tile, SLOT, tile), BF16),
            pltpu.VMEM((seq, SLOT), BF16),
        ],
        compiler_params=pltpu.CompilerParams(vmem_limit_bytes=VMEM_LIMIT),
        cost_estimate=pl.CostEstimate(
            flops=4 * seq * seq * SLOT, bytes_accessed=8 * seq * SLOT, transcendentals=seq * seq
        ),
        name="attend_forward",
    )(order, queries, keys, values)


def attend_backward(order, queries, keys, values, grads, mixed, lse, blk):
    seq = queries.shape[0]
    tile = tile_of(seq)
    tiles = seq // tile
    return pl.pallas_call(
        functools.partial(backward_kernel, blk=blk, tile=tile),
        out_shape=(
            jax.ShapeDtypeStruct((seq, 3 * SLOT), BF16),
            jax.ShapeDtypeStruct((8, SLOT), F32),
        ),
        in_specs=[SMEM_SPEC] + [VMEM_SPEC] * 6,
        out_specs=(VMEM_SPEC, VMEM_SPEC),
        scratch_shapes=[
            pltpu.VMEM((2, seq, SLOT), BF16),
            pltpu.VMEM((seq, SLOT), BF16),
            pltpu.VMEM((seq, SLOT), BF16),
            pltpu.VMEM((2, seq, SLOT), BF16),
            pltpu.VMEM((seq, SLOT), F32),
            pltpu.VMEM((tiles, SLOT, tile), BF16),
            pltpu.VMEM((tiles, SLOT, tile), F32),
            pltpu.VMEM((tiles, 8, tile), F32),
            pltpu.VMEM((tile, SLOT), F32),
            pltpu.VMEM((tile, SLOT), F32),
            pltpu.VMEM((3, seq, SLOT), BF16),
        ],
        compiler_params=pltpu.CompilerParams(vmem_limit_bytes=VMEM_LIMIT),
        cost_estimate=pl.CostEstimate(
            flops=10 * seq * seq * SLOT, bytes_accessed=20 * seq * SLOT, transcendentals=seq * seq
        ),
        name="attend_backward",
    )(order, queries, keys, values, grads, mixed, lse)


def body(
    tokens,
    cotangent,
    block_order,
    ln1_gain,
    ln1_bias,
    w_qkv,
    qv_bias,
    w_out,
    out_bias,
    ln2_gain,
    ln2_bias,
    w_fc,
    fc_bias,
    w_proj,
    proj_bias,
):
    width = HEADS * HEAD_DIM
    half = width // 2
    count = lax.axis_size("context")
    rows = tokens.shape[1]
    seq = count * rows
    blk = rows // 2
    hidden = fc_bias.shape[0] * 2
    share = hidden // count
    own_rows = w_qkv.shape[0]
    padded = count * SLOT
    grad_scale = 1.0 / math.sqrt(lax.axis_size("fsdp") * seq)
    side = lax.axis_index("fsdp")
    ring = Ring(count)
    mine = ring.mine
    order = block_order.astype(jnp.int32)

    vectors = jnp.concatenate(
        [
            jnp.stack(
                [ln1_gain, ln1_bias, qv_bias[:, 0], qv_bias[:, 1], out_bias, ln2_gain, ln2_bias, proj_bias]
            ),
            fc_bias.reshape(-1, half),
        ],
        axis=0,
    )
    low, high = pair_halves(vectors, side)
    wide = jnp.concatenate([low[:8], high[:8]], axis=1).astype(F32)
    gain_one, shift_one, q_bias, v_bias, out_b, gain_two, shift_two, proj_b = [wide[i] for i in range(8)]
    fc_b = jnp.concatenate([low[8:].reshape(-1), high[8:].reshape(-1)])
    fc_b = lax.dynamic_slice(fc_b, (mine * share,), (share,)).astype(F32)
    slot_bias = jnp.stack([q_bias, jnp.zeros_like(q_bias), v_bias])
    slot_bias = jnp.pad(slot_bias, ((0, 0), (0, padded - width))).reshape(3, count, SLOT)
    slot_bias = lax.dynamic_index_in_dim(slot_bias, mine, axis=1, keepdims=False).reshape(3 * SLOT)

    xs16 = tokens[0]
    xs = xs16.astype(F32)
    buffers = {}

    def put(name):
        def place(device, piece, first):
            value = piece
            if name == "h_one":
                normed, _ = norm_stats(piece.astype(F32))
                value = (normed * gain_one + shift_one).astype(BF16)
            if name not in buffers:
                buffers[name] = jnp.zeros((count, 2, blk, width), BF16)
            buffers[name] = lax.dynamic_update_slice(
                buffers[name], value[None], (device, jnp.int32(first), jnp.int32(0), jnp.int32(0))
            )

        return place

    ring.gather(xs16.reshape(2, blk, width), put("h_one"))
    h_one_all = buffers["h_one"].reshape(seq, width)
    normed_one, inv_one = norm_stats(xs)

    low, high = pair_halves(w_qkv, side)
    parts = jnp.concatenate([low, high], axis=1).reshape(own_rows, 3, width)
    parts = jnp.pad(parts, ((0, 0), (0, 0), (0, padded - width))).reshape(own_rows, 3, count, SLOT)
    parts = parts.transpose(2, 0, 1, 3).reshape(count, own_rows, 3 * SLOT)
    w_heads = lax.all_to_all(parts, "context", 0, 0, tiled=True).reshape(width, 3 * SLOT)

    qkv = jnp.dot(h_one_all, w_heads, preferred_element_type=F32) + slot_bias
    qkv = qkv.astype(BF16)
    queries, keys, values = qkv[:, :SLOT], qkv[:, SLOT : 2 * SLOT], qkv[:, 2 * SLOT :]

    w_out_b, cot_b, h_one_b = lax.optimization_barrier((w_out, cotangent, h_one_all))
    low, high = pair_halves(w_out_b, side)
    w_out_all = lax.all_gather(jnp.concatenate([low, high], axis=1), "context", axis=0, tiled=True)
    cot16 = cot_b[0]
    cot_all = lax.all_gather(cot16, "context", axis=0, tiled=True)

    low, high = pair_halves(w_fc, side)
    parts = jnp.concatenate([low, high], axis=1).reshape(own_rows, count, share).transpose(1, 0, 2)
    w_fc_part = lax.all_to_all(parts, "context", 0, 0, tiled=True).reshape(width, share)
    low, high = pair_halves(w_proj, side)
    w_proj_part = jnp.concatenate([low, high], axis=1)

    mixed, lse = attend_forward(order, queries, keys, values, blk)
    attn_out = lax.all_to_all(mixed, "context", 0, 1, tiled=True)[:, :width]

    resid_one = xs + jnp.dot(attn_out, w_out_all, preferred_element_type=F32) + out_b
    normed_two, inv_two = norm_stats(resid_one)
    h_two = (normed_two * gain_two + shift_two).astype(BF16)
    ring.gather(h_two.reshape(2, blk, width), put("h_two"))
    h_two_all = buffers["h_two"].reshape(seq, width)

    grad_act = dot_nt(cot_all, w_proj_part)
    pre_act = jnp.dot(h_two_all, w_fc_part, preferred_element_type=F32) + fc_b
    act_value, act_slope = gelu_pair(pre_act)
    act_half = act_value.astype(BF16)
    grad_pre = grad_act * act_slope
    g_fc_bias = jnp.sum(grad_pre, axis=0)
    grad_pre16 = grad_pre.astype(BF16)
    h2_terms = dot_nt(grad_pre16, w_fc_part).astype(BF16).reshape(count, 2, blk, width)

    def taker(terms):
        return lambda device: lax.dynamic_index_in_dim(terms, device, axis=0, keepdims=False)

    grad_h2 = ring.scatter(taker(h2_terms)).reshape(rows, width)

    grad_y = cotangent[0].astype(F32)
    grad_r1 = grad_y + norm_back(grad_h2, normed_two, inv_two, gain_two)
    grad_r16 = grad_r1.astype(BF16)
    grad_o16 = dot_nt(grad_r16, w_out_all).astype(BF16)
    grad_heads = lax.all_to_all(
        jnp.pad(grad_o16, ((0, 0), (0, padded - width))), "context", 1, 0, tiled=True
    )

    act_b, grad_heads_b = lax.optimization_barrier((act_half, grad_heads))
    out_terms = jnp.dot(act_b, w_proj_part, preferred_element_type=F32).astype(BF16)
    out_sum = ring.scatter(taker(out_terms.reshape(count, 2, blk, width))).reshape(rows, width)
    result = (resid_one + out_sum + proj_b).astype(BF16)

    g_proj = lax.dot_general(act_b, cot_all, (((0,), (0,)), ((), ())), preferred_element_type=F32) * grad_scale
    g_w_proj = pair_sum(g_proj[:, :half], g_proj[:, half:], side)

    g_fc = lax.dot_general(h_two_all, grad_pre16, (((0,), (0,)), ((), ())), preferred_element_type=F32)
    g_fc = (g_fc * grad_scale).astype(BF16).reshape(count, own_rows, share)
    g_fc = lax.all_to_all(g_fc, "context", 0, 0, tiled=True)
    g_fc = g_fc.transpose(1, 0, 2).reshape(own_rows, hidden)
    g_w_fc = pair_sum(g_fc[:, : hidden // 2], g_fc[:, hidden // 2 :], side)

    g_out = lax.dot_general(attn_out, grad_r16, (((0,), (0,)), ((), ())), preferred_element_type=F32) * grad_scale
    g_out = pair_sum(g_out[:, :half], g_out[:, half:], side).astype(BF16).reshape(count, own_rows, half)
    even = own_rows + own_rows % 2
    g_out = jnp.pad(g_out, ((0, 0), (0, even - own_rows), (0, 0))).reshape(count, 2, even // 2, half)
    g_w_out = ring.scatter(taker(g_out)).reshape(even, half)[:own_rows]

    grad_qkv16, head_sums = attend_backward(order, queries, keys, values, grad_heads, mixed, lse, blk)
    h1_terms = dot_nt(grad_qkv16, w_heads).astype(BF16).reshape(count, 2, blk, width)
    grad_h1 = ring.scatter(taker(h1_terms)).reshape(rows, width)
    grad_x = (grad_r1 + norm_back(grad_h1, normed_one, inv_one, gain_one)).astype(BF16)

    g_qkv = lax.dot_general(h_one_all, grad_qkv16, (((0,), (0,)), ((), ())), preferred_element_type=F32)
    g_qkv = (g_qkv * grad_scale).astype(BF16).reshape(count, own_rows, 3 * SLOT)
    g_qkv = lax.all_to_all(g_qkv, "context", 0, 0, tiled=True)
    g_qkv = g_qkv.reshape(count, own_rows, 3, SLOT).transpose(1, 2, 0, 3)
    g_qkv = g_qkv.reshape(own_rows, 3, padded)[:, :, :width].reshape(own_rows, 3 * width)
    g_w_qkv = pair_sum(g_qkv[:, : 3 * half], g_qkv[:, 3 * half :], side)

    fc_place = lax.dynamic_update_slice(jnp.zeros((hidden,), F32), g_fc_bias, (mine * share,))
    early = jnp.concatenate(
        [
            jnp.sum(grad_h2 * normed_two, axis=0),
            jnp.sum(grad_h2, axis=0),
            jnp.sum(grad_r1, axis=0),
            jnp.sum(grad_y, axis=0),
            fc_place,
        ]
    )
    early = sum_everywhere(early.reshape(-1, SLOT) * grad_scale, count).reshape(-1)
    head_place = lax.dynamic_update_slice(
        jnp.zeros((2, padded), F32), head_sums[:2], (jnp.int32(0), mine * SLOT)
    )[:, :width]
    late = jnp.concatenate(
        [jnp.sum(grad_h1 * normed_one, axis=0), jnp.sum(grad_h1, axis=0), head_place[0], head_place[1]]
    )
    late = sum_everywhere(late.reshape(-1, SLOT) * grad_scale, count).reshape(-1)

    def own_half(vector):
        return lax.dynamic_slice(vector, (side * (vector.shape[0] // 2),), (vector.shape[0] // 2,))

    g_ln2_gain, g_ln2_bias, g_out_bias, g_proj_bias = [
        own_half(early[i * width : (i + 1) * width]) for i in range(4)
    ]
    g_fc_bias = own_half(early[4 * width :])
    g_ln1_gain, g_ln1_bias, g_q, g_v = [own_half(late[i * width : (i + 1) * width]) for i in range(4)]
    return (
        result[None],
        grad_x[None],
        g_ln1_gain,
        g_ln1_bias,
        g_w_qkv,
        jnp.stack([g_q, g_v], axis=1),
        g_w_out,
        g_out_bias,
        g_ln2_gain,
        g_ln2_bias,
        g_w_fc,
        g_fc_bias,
        g_w_proj,
        g_proj_bias,
    )


def solution(mesh):
    rows = P("fsdp", "context", None)
    weight = P("context", "fsdp")
    vector = P("fsdp")
    pair = P("fsdp", None)
    return jax.shard_map(
        body,
        mesh=mesh,
        in_specs=(
            rows, rows, P(), vector, vector, weight, pair, weight,
            vector, vector, vector, weight, vector, weight, vector,
        ),
        out_specs=(
            rows, rows, vector, vector, weight, pair, weight,
            vector, vector, vector, weight, vector, weight, vector,
        ),
        check_vma=False,
    )
```

```python
import functools
import math

import jax
import jax.numpy as jnp
from jax import lax
from jax.experimental import pallas as pl
from jax.experimental.pallas import tpu as pltpu
from jax.sharding import PartitionSpec as P

HEADS = 25
HEAD_DIM = 64
SLOT = 2 * HEAD_DIM

EPSILON = 1e-05
GELU_ROOT = math.sqrt(2.0 / math.pi)
GELU_CUBIC = 0.044715
NEG_LARGE = -1e30
SCALE = HEAD_DIM ** (-0.5)
VMEM_LIMIT = 56 * 1024 * 1024
F32 = jnp.float32
BF16 = jnp.bfloat16


def norm_stats(values):
    centred = values - jnp.mean(values, axis=-1, keepdims=True)
    inv_std = lax.rsqrt(jnp.mean(centred * centred, axis=-1, keepdims=True) + EPSILON)
    return centred * inv_std, inv_std


def norm_back(upstream, normed, inv_std, gain_vec):
    scaled = upstream * gain_vec
    return inv_std * (
        scaled
        - jnp.mean(scaled, axis=-1, keepdims=True)
        - normed * jnp.mean(scaled * normed, axis=-1, keepdims=True)
    )


def gelu_pair(pre_act):
    inner = GELU_ROOT * (pre_act + GELU_CUBIC * pre_act * pre_act * pre_act)
    tangent = jnp.tanh(inner)
    act_value = 0.5 * pre_act * (1.0 + tangent)
    act_slope = 0.5 * (1.0 + tangent) + 0.5 * pre_act * (1.0 - tangent * tangent) * GELU_ROOT * (
        1.0 + 3.0 * GELU_CUBIC * pre_act * pre_act
    )
    return (act_value, act_slope)


class Ring:
    def __init__(self, count):
        chips = count // 2
        self.count, self.size, self.far = count, chips, chips // 2
        self.mine = lax.axis_index("context")
        self.core = self.mine % 2
        chip = self.mine // 2
        if chips == 8:
            order = [0, 2, 4, 6, 7, 5, 3, 1]
            self.place = jnp.where(chip % 2 == 0, chip // 2, (15 - chip) // 2)
        else:
            order = list(range(chips))
            self.place = chip
        self.spot = jnp.stack([self.place, self.core]).astype(jnp.int32)
        self.links = []
        for i in range(chips):
            self.links.append((2 * order[i], 2 * order[(i + 1) % chips]))
            self.links.append((2 * order[i] + 1, 2 * order[(i - 1) % chips] + 1))
        self.swaps = [(i, i ^ 1) for i in range(count)]

    def layout(self):
        steps = [[(0, None)]] + [[(step, None), (-step, None)] for step in range(1, self.far)]
        return steps + [[(self.far, 0), (self.far, 1)]]

    def swap(self, value):
        return lax.ppermute(value, "context", self.swaps)

    def send(self, value):
        return lax.ppermute(value, "context", self.links)

    def own(self, value, other=0):
        rows = value.shape[0] // 2
        return lax.dynamic_slice_in_dim(value, (self.core ^ other) * rows, rows)

    def gather(self, block, visit, hold=None):
        other = self.swap(block)
        current = jnp.concatenate(
            [jnp.where(self.core == 0, block, other), jnp.where(self.core == 0, other, block)], axis=0
        )
        events = [visit(0, [current])]
        for step in range(1, self.far + 1):
            if step == self.far:
                current = self.own(current)
            if step >= 2:
                current = after(current, events[step - 2])
            if hold is not None:
                current = hold(step, current)
            current = self.send(current)
            events.append(visit(step, [current, self.swap(current)]))

    def pick(self, array):
        cut = array.shape[1] // 2
        steps = []
        for entries in self.layout():
            blocks = []
            for offset, other in entries:
                first, size = (0, 2 * cut) if other is None else ((self.core ^ other) * cut, cut)
                chip = device_at(self.size, self.spot, offset, None) // 2
                blocks.append(lax.dynamic_slice(array, (chip, first, 0), (1, size, array.shape[2]))[0])
            steps.append(blocks)
        return steps

    def scatter(self, give, hold=None):
        sent = None
        for step in range(self.far, 0, -1):
            first, second = give(step, sent)
            if step == self.far:
                value = total([first, self.swap(second)])
            else:
                value = total([second, self.swap(first)])
            if step == self.far - 1:
                got = got.astype(F32)
                blank = jnp.zeros_like(got)
                value = value + jnp.concatenate(
                    [jnp.where(self.core == 0, got, blank), jnp.where(self.core == 0, blank, got)], axis=0
                )
            elif step < self.far - 1:
                value = value + got.astype(F32)
            sent = value.astype(BF16)
            if hold is not None:
                sent = hold(step, sent)
            got = self.send(sent)
        value = total([give(0, sent)[0], got])
        return self.own(value) + self.swap(self.own(value, 1).astype(BF16)).astype(F32)


def device_at(size, spot, offset, other):
    place, core = spot[0], spot[1]
    at = lax.rem(place + offset * (2 * core - 1) + size, size)
    chip = jnp.where(at < 4, 2 * at, 15 - 2 * at) if size == 8 else at
    return 2 * chip if other is None else 2 * chip + (core ^ other)


def wide(value, axis=-1):
    axis %= value.ndim
    more = -value.shape[axis] % 128
    return jnp.pad(value, [(0, more if i == axis else 0) for i in range(value.ndim)])


def total(values):
    result = values[0].astype(F32)
    for value in values[1:]:
        result = result + value.astype(F32)
    return result


def after(value, *events):
    return lax.optimization_barrier((value,) + events)[0]


def cross(value):
    return lax.ppermute(value, "fsdp", [(0, 1), (1, 0)])


def pair_halves(own, side):
    got = cross(own)
    return jnp.where(side == 0, own, got), jnp.where(side == 0, got, own)


def pair_sum(left, right, side):
    got = cross(jnp.where(side == 0, right, left).astype(BF16))
    return jnp.where(side == 0, left, right).astype(F32) + got.astype(F32)


def sum_everywhere(value, count):
    step = 1
    while step < count:
        value = value + lax.ppermute(value, "context", [(i, i ^ step) for i in range(count)])
        step *= 2
    return value + cross(value)


def even_rows(value, axis=0):
    odd = value.shape[axis] % 2
    if not odd:
        return value
    return jnp.pad(value, [(0, odd if i == axis else 0) for i in range(value.ndim)])


def spread(value):
    return lax.all_to_all(value, "context", 0, 0, tiled=True)


def start_fc(w_fc, side, count, share):
    w_fc = even_rows(w_fc)
    cut = w_fc.shape[0] // 2
    mine, got = w_fc[:cut], cross(w_fc[cut:])
    blocks = jnp.concatenate([jnp.where(side == 0, mine, got), jnp.where(side == 0, got, mine)], axis=1)
    return blocks.reshape(cut, count, share).transpose(1, 0, 2)


def finish_fc(landed, side, upper, rows):
    other = cross(landed)
    is_first = upper == side
    both = jnp.concatenate(
        [jnp.where(is_first, landed, other), jnp.where(is_first, other, landed)], axis=1
    )
    return both[:, :rows].reshape(landed.shape[0] * rows, landed.shape[2])


def return_fc(grad, side, upper, count, share, rows):
    grad = even_rows(grad.reshape(count, rows, share), 1)
    cut = grad.shape[1] // 2
    first, second = grad[:, :cut], grad[:, cut:]
    is_first = upper == side
    got = cross(jnp.where(is_first, second, first))
    landed = spread(total([jnp.where(is_first, first, second), got]).astype(BF16))
    low, high = landed[: count // 2], landed[count // 2 :]
    mine, got = jnp.where(side == 0, low, high), cross(jnp.where(side == 0, high, low))
    both = jnp.concatenate([mine, got], axis=1).astype(F32).transpose(1, 0, 2)
    return both.reshape(2 * cut, count // 2 * share)[:rows]


def start_heads(w_qkv, side, count):
    rows, width = w_qkv.shape[0], w_qkv.shape[1] * 2 // 3
    half = width // 2
    main = jnp.where(side == 0, w_qkv[:, :width], w_qkv[:, half:])
    keys = even_rows(jnp.where(side == 0, w_qkv[:, width:], w_qkv[:, :half]))
    cut = keys.shape[0] // 2
    first, second = keys[:cut], keys[cut:]
    got = cross(jnp.where(side == 0, second, first))
    keys = jnp.concatenate([jnp.where(side == 0, first, got), jnp.where(side == 0, got, second)], axis=1)
    blocks = jnp.pad(jnp.concatenate([main, keys], axis=0), ((0, 0), (0, count * SLOT - width)))
    return blocks.reshape(rows + cut, count, SLOT).transpose(1, 0, 2)


def finish_heads(landed, side, rows, width):
    other = cross(landed)
    one, two = jnp.where(side == 0, landed, other), jnp.where(side == 0, other, landed)
    keys = jnp.concatenate([one[:, rows:], two[:, rows:]], axis=1)[:, :rows]
    heads = jnp.concatenate([one[:, :rows], keys, two[:, :rows]], axis=2)
    return heads.reshape(width, 3 * SLOT)


def return_heads(grad, side, count, rows, width):
    half = width // 2
    grad = grad.reshape(count, rows, 3 * SLOT)
    keys = even_rows(grad[:, :, SLOT : 2 * SLOT], 1)
    cut = keys.shape[1] // 2
    one = jnp.concatenate([grad[:, :, :SLOT], keys[:, :cut]], axis=1)
    two = jnp.concatenate([grad[:, :, 2 * SLOT :], keys[:, cut:]], axis=1)
    got = cross(jnp.where(side == 0, two, one))
    landed = spread(total([jnp.where(side == 0, one, two), got]).astype(BF16))
    landed = landed.transpose(1, 0, 2).reshape(rows + cut, count * SLOT)[:, :width]
    main, keys = landed[:rows], landed[rows:]
    low, high = keys[:, :half], keys[:, half:]
    got, own = cross(jnp.where(side == 0, high, low)), jnp.where(side == 0, low, high)
    keys = jnp.concatenate([jnp.where(side == 0, own, got), jnp.where(side == 0, got, own)], axis=0)[:rows]
    return jnp.where(
        side == 0, jnp.concatenate([main, keys], axis=1), jnp.concatenate([keys, main], axis=1)
    ).astype(F32)


def dot_nt(first, second):
    return lax.dot_general(first, second, (((1,), (1,)), ((), ())), preferred_element_type=F32)


def dot_nn(first, second):
    return lax.dot_general(first, second, (((1,), (0,)), ((), ())), preferred_element_type=F32)


def dot_tn(first, second):
    return lax.dot_general(first, second, (((0,), (0,)), ((), ())), preferred_element_type=F32)


VMEM_SPEC = pl.BlockSpec(memory_space=pltpu.VMEM)
SMEM_SPEC = pl.BlockSpec(memory_space=pltpu.SMEM)
ANY_SPEC = pl.BlockSpec(memory_space=pl.ANY)


def local_call(kernel, name, outs, ins, args, flops, scratch=(), exps=0):
    moved = sum(math.prod(x.shape) * x.dtype.itemsize for x in list(args) + list(outs))
    return pl.pallas_call(
        kernel,
        out_shape=tuple(outs),
        in_specs=list(ins),
        out_specs=tuple(VMEM_SPEC for _ in outs),
        scratch_shapes=list(scratch),
        compiler_params=pltpu.CompilerParams(vmem_limit_bytes=VMEM_LIMIT),
        cost_estimate=pl.CostEstimate(flops=flops, bytes_accessed=moved, transcendentals=exps),
        name=name,
    )(*args)


def shape_of(rows, cols, kind):
    return jax.ShapeDtypeStruct((rows, cols), kind)


def norm_blocks(blocks, gain, shift, width):
    count = len(blocks)

    def kernel(*refs):
        ins, gain_ref, shift_ref, outs = refs[:count], refs[count], refs[count + 1], refs[count + 2 :]
        for i in range(count):
            values = ins[i][...].astype(F32)
            lane = lax.broadcasted_iota(jnp.int32, (1, values.shape[1]), 1)
            centred = values - jnp.sum(values, axis=-1, keepdims=True) * (1.0 / width)
            centred = jnp.where(lane < width, centred, 0.0)
            spread_of = jnp.sum(centred * centred, axis=-1, keepdims=True) * (1.0 / width)
            normed = centred * lax.rsqrt(spread_of + EPSILON)
            outs[i][...] = (normed * gain_ref[...] + shift_ref[...]).astype(BF16)
            outs[count + i][...] = normed.astype(BF16)

    outs = [jax.ShapeDtypeStruct(x.shape, BF16) for x in blocks] * 2
    args = list(blocks) + [gain, shift]
    size = sum(x.size for x in blocks)
    result = local_call(kernel, "norm_blocks", outs, [VMEM_SPEC] * len(args), args, 10 * size)
    return list(result[:count]), list(result[count:])


def feed_blocks(spot, blocks, cot_all, w_fc, w_proj, bias, size, entries):
    count, (width, share) = len(blocks), w_fc.shape
    sizes = [x.shape[0] for x in blocks]
    rows = sum(sizes)
    unit = sizes[0] // 2 if entries[0][1] is None else sizes[0]

    def kernel(*refs):
        spot_ref, cot_ref, h_refs = refs[0], refs[1], refs[2 : 2 + count]
        fc_ref, proj_ref, bias_ref, act_ref, du_ref, sum_ref = refs[2 + count : 8 + count]
        outs, cots, sems = refs[8 + count : -2], refs[-2], refs[-1]
        copies, at = [], 0
        for i, (offset, other) in enumerate(entries):
            device = device_at(size, spot_ref, offset, other)
            rows_there = pl.ds(pl.multiple_of(device * unit, unit), sizes[i])
            copy = pltpu.make_async_copy(cot_ref.at[rows_there, :], cots.at[pl.ds(at, sizes[i]), :], sems.at[i])
            copy.start()
            copies.append(copy)
            at += sizes[i]
        rows_in = jnp.concatenate([h_refs[i][...] for i in range(count)], axis=0)
        act, slope = gelu_pair(dot_nn(rows_in, fc_ref[...]) + bias_ref[...])
        act_ref[...] = act.astype(BF16)
        for copy in copies:
            copy.wait()
        grad = dot_nt(cots[...], proj_ref[...]) * slope
        sum_ref[...] = jnp.sum(grad, axis=0, keepdims=True)
        grad = grad.astype(BF16)
        du_ref[...] = grad
        terms = dot_nt(grad, fc_ref[...]).astype(BF16)
        at = 0
        for i in range(count):
            outs[i][...] = terms[at : at + sizes[i]]
            at += sizes[i]

    outs = [shape_of(rows, share, BF16), shape_of(rows, share, BF16), shape_of(1, share, F32)]
    outs += [shape_of(size, width, BF16) for size in sizes]
    args = [spot, cot_all] + list(blocks) + [w_fc, w_proj, bias]
    ins = [SMEM_SPEC, ANY_SPEC] + [VMEM_SPEC] * (count + 3)
    scratch = [pltpu.VMEM((rows, width), BF16), pltpu.SemaphoreType.DMA((count,))]
    result = local_call(
        kernel, "feed_blocks", outs, ins, args, 6 * rows * width * share, scratch, rows * share
    )
    return result[0], result[1], result[2], list(result[3:])


def project_blocks(act, w_proj, sizes):
    width = w_proj.shape[1]

    def kernel(act_ref, proj_ref, *outs):
        terms = dot_nn(act_ref[...], proj_ref[...]).astype(BF16)
        at = 0
        for i, size in enumerate(sizes):
            outs[i][...] = terms[at : at + size]
            at += size

    outs = [shape_of(size, width, BF16) for size in sizes]
    result = local_call(
        kernel, "project_blocks", outs, [VMEM_SPEC] * 2, [act, w_proj], 2 * act.size * width
    )
    return list(result)


def input_blocks(grad, w_heads, normed):
    count, width = len(normed), w_heads.shape[0]
    sizes = [x.shape[0] for x in normed]

    def kernel(*refs):
        grad_ref, w_ref, n_refs, sum_ref, outs = refs[0], refs[1], refs[2 : 2 + count], refs[2 + count], refs[3 + count :]
        terms = dot_nt(grad_ref[...], w_ref[...])
        gains = jnp.zeros((1, width), F32)
        at = 0
        for i, size in enumerate(sizes):
            term = terms[at : at + size]
            at += size
            outs[i][...] = term.astype(BF16)
            gains += jnp.sum(term * n_refs[i][...].astype(F32), axis=0, keepdims=True)
        sum_ref[0:1, :] = gains
        sum_ref[1:2, :] = jnp.sum(terms, axis=0, keepdims=True)

    outs = [shape_of(2, width, F32)] + [shape_of(size, width, BF16) for size in sizes]
    args = [grad, w_heads] + list(normed)
    result = local_call(
        kernel, "input_blocks", outs, [VMEM_SPEC] * len(args), args, 2 * grad.size * width
    )
    return result[0], list(result[1:])


def pack(spot, groups, layout, size, seq):
    flat, plan = [], []
    for index, steps in enumerate(groups):
        for blocks, entries in zip(steps, layout):
            blocks = blocks if isinstance(blocks, list) else [blocks]
            at = 0
            for i, (offset, other) in enumerate(entries):
                rows = 2 * seq // (2 * size) if other is None else seq // (2 * size)
                if len(blocks) == len(entries):
                    plan.append((index, len(flat) + i, 0, rows, offset, other))
                else:
                    plan.append((index, len(flat), at, rows, offset, other))
                at += rows
            flat += blocks
    unit = seq // (2 * size)

    def kernel(*refs):
        spot_ref, ins = refs[0], refs[1 : 1 + len(flat)]
        outs, sems = refs[1 + len(flat) : -1], refs[-1]
        copies = []
        for i, (index, source, first, rows, offset, other) in enumerate(plan):
            device = device_at(size, spot_ref, offset, other)
            there = pl.ds(pl.multiple_of(device * unit, unit), rows)
            copy = pltpu.make_async_copy(
                ins[source].at[pl.ds(first, rows), :], outs[index].at[there, :], sems.at[i]
            )
            copy.start()
            copies.append(copy)
        for copy in copies:
            copy.wait()

    outs = []
    for steps in groups:
        sample = steps[0][0] if isinstance(steps[0], list) else steps[0]
        outs.append(shape_of(seq, sample.shape[1], sample.dtype))
    moved = sum(2 * math.prod(x.shape) * x.dtype.itemsize for x in outs)
    return pl.pallas_call(
        kernel,
        out_shape=tuple(outs),
        in_specs=[SMEM_SPEC] + [ANY_SPEC] * len(flat),
        out_specs=tuple(VMEM_SPEC for _ in outs),
        scratch_shapes=[pltpu.SemaphoreType.DMA((len(plan),))],
        compiler_params=pltpu.CompilerParams(vmem_limit_bytes=VMEM_LIMIT),
        cost_estimate=pl.CostEstimate(flops=0, bytes_accessed=moved, transcendentals=0),
        name="pack",
    )(spot, *flat)


def head_masks(scale):
    lane = lax.broadcasted_iota(jnp.int32, (1, SLOT), 1)
    return [jnp.where(lane < HEAD_DIM, scale, 0.0), jnp.where(lane < HEAD_DIM, 0.0, scale)]


def flipped(value):
    return value.astype(F32).T


def causal(tile):
    keys = lax.broadcasted_iota(jnp.int32, (tile, tile), 0)
    queries = lax.broadcasted_iota(jnp.int32, (tile, tile), 1)
    return keys <= queries


def span(index, size):
    return pl.ds(pl.multiple_of(index * size, size), size)


def tile_of(seq):
    return math.gcd(seq, 512)


def attend_forward(order, spot, blocks, w_heads, bias, layout, blk):
    size = len(layout) - 1
    chips = 2 * size
    seq = 4 * chips * blk
    width = w_heads.shape[0]
    tile = tile_of(seq)
    tiles = seq // tile
    flat = [(step, entry) for step, entries in enumerate(layout) for entry in entries]
    pieces = len(flat)

    def kernel(*refs):
        order_ref, spot_ref = refs[:2]
        h_refs = refs[2 : 2 + pieces]
        w_ref, bias_ref, o_ref, lse_ref, qs, ks, vs, held, vt, os, sems = refs[2 + pieces :]
        masks = head_masks(SCALE)
        copies, starts, at = [], [], 0
        for i in range(pieces):
            rows = h_refs[i].shape[0]
            copy = pltpu.make_async_copy(h_refs[i], held.at[pl.ds(at, rows), :], sems.at[i])
            copy.start()
            copies.append(copy)
            starts.append(at)
            at += rows

        index = 0
        for step, entries in enumerate(layout):
            first = starts[index]
            for i in range(len(entries)):
                copies[index + i].wait()
            rows = sum(h_refs[index + i].shape[0] for i in range(len(entries)))
            mixed = dot_nn(held[first : first + rows, :], w_ref[...]) + bias_ref[...]
            for i, (offset, other) in enumerate(entries):
                base = starts[index + i] - first
                device = device_at(chips, spot_ref, offset, other)
                for part in range(4 if other is None else 2):
                    there = span(order_ref[2 * device + part], blk)
                    block = mixed[base : base + blk].astype(BF16)
                    base += blk
                    query = block[:, :SLOT].astype(F32)
                    for head in range(2):
                        qs[head, there, :] = (query * masks[head]).astype(BF16)
                    ks[there, :] = block[:, SLOT : 2 * SLOT]
                    vs[there, :] = block[:, 2 * SLOT :]
            index += len(entries)

        def turn(t, carry):
            vt[t] = flipped(vs[span(t, tile), :]).astype(BF16)
            return carry

        lax.fori_loop(0, tiles, turn, 0)
        visible = causal(tile)

        def query_tile(i, carry):
            def key_tile(j, state, diagonal):
                fresh = []
                for head in range(2):
                    top, sums, accum = state[3 * head : 3 * head + 3]
                    scores = dot_nt(ks[span(j, tile), :], qs[head, span(i, tile), :])
                    if diagonal:
                        scores = jnp.where(visible, scores, NEG_LARGE)
                    new_top = jnp.maximum(top, jnp.max(scores, axis=0, keepdims=True))
                    terms = jnp.exp(scores - new_top)
                    decay = jnp.exp(top - new_top)
                    sums = sums * decay + jnp.sum(terms, axis=0, keepdims=True)
                    values = vt[j, head * HEAD_DIM : (head + 1) * HEAD_DIM, :]
                    accum = accum * decay + dot_nn(values, terms.astype(BF16))
                    fresh += [new_top, sums, accum]
                return tuple(fresh)

            start = (
                jnp.full((1, tile), NEG_LARGE, F32),
                jnp.zeros((1, tile), F32),
                jnp.zeros((HEAD_DIM, tile), F32),
            )
            state = lax.fori_loop(0, i, lambda j, state: key_tile(j, state, False), start + start)
            state = key_tile(i, state, True)
            mixed = jnp.concatenate([state[2] / state[1], state[5] / state[4]], axis=0)
            os[span(i, tile), :] = mixed.T.astype(BF16)
            for head in range(2):
                lse_ref[i, head : head + 1, :] = state[3 * head] + jnp.log(state[3 * head + 1])
            return carry

        lax.fori_loop(0, tiles, query_tile, 0)

        def sort_out(s, carry):
            o_ref[span(s, blk), :] = os[span(order_ref[s], blk), :]
            return carry

        lax.fori_loop(0, seq // blk, sort_out, 0)

    outs = [
        shape_of(seq, SLOT, BF16),
        jax.ShapeDtypeStruct((tiles, 8, tile), F32),
        jax.ShapeDtypeStruct((2, seq, SLOT), BF16),
        shape_of(seq, SLOT, BF16),
        shape_of(seq, SLOT, BF16),
    ]
    scratch = [
        pltpu.VMEM((seq, width), BF16),
        pltpu.VMEM((tiles, SLOT, tile), BF16),
        pltpu.VMEM((seq, SLOT), BF16),
        pltpu.SemaphoreType.DMA((pieces,)),
    ]
    args = [order, spot] + [block for step in blocks for block in step] + [w_heads, bias]
    ins = [SMEM_SPEC] * 2 + [ANY_SPEC] * pieces + [VMEM_SPEC] * 2
    flops = 4 * seq * seq * SLOT + 6 * seq * width * SLOT
    return local_call(kernel, "attend_forward", outs, ins, args, flops, scratch, seq * seq)


def attend_backward(order, spot, saved, grads, mixed, lse, layout, blk):
    queries, keys, values = saved
    seq = keys.shape[0]
    chips = 2 * (len(layout) - 1)
    tile = tile_of(seq)
    tiles = seq // tile
    steps = len(layout)

    def kernel(order_ref, spot_ref, qs, ks, vs, g_ref, o_ref, lse_ref, sum_ref, *refs):
        d_refs = refs[:steps]
        gs, ps, kt, dqt, drow, dk, dv, dsort = refs[steps:]
        g_masks = head_masks(1.0)

        def sort_in(s, carry):
            here, there = span(s, blk), span(order_ref[s], blk)
            g_block = g_ref[here, :].astype(F32)
            for head in range(2):
                gs[head, there, :] = (g_block * g_masks[head]).astype(BF16)
            ps[there, :] = g_block * o_ref[here, :].astype(F32)
            return carry

        lax.fori_loop(0, seq // blk, sort_in, 0)

        def turn(t, carry):
            kt[t] = flipped(ks[span(t, tile), :]).astype(BF16)
            products = ps[span(t, tile), :].T
            for head in range(2):
                drow[t, head : head + 1, :] = jnp.sum(
                    products[head * HEAD_DIM : (head + 1) * HEAD_DIM], axis=0, keepdims=True
                )
            dqt[t] = jnp.zeros((SLOT, tile), F32)
            return carry

        lax.fori_loop(0, tiles, turn, 0)
        visible = causal(tile)
        sum_ref[...] = jnp.zeros(sum_ref.shape, F32)

        def key_tile(j, carry):
            dk[...] = jnp.zeros(dk.shape, F32)
            dv[...] = jnp.zeros(dv.shape, F32)

            def query_tile(i, diagonal):
                key_add, value_add = [], []
                for head in range(2):
                    scores = dot_nt(ks[span(j, tile), :], qs[head, span(i, tile), :])
                    terms = jnp.exp(scores - lse_ref[i, head : head + 1, :])
                    if diagonal:
                        terms = jnp.where(visible, terms, 0.0)
                    slopes = dot_nt(vs[span(j, tile), :], gs[head, span(i, tile), :])
                    slopes = (terms * (slopes - drow[i, head : head + 1, :])).astype(BF16)
                    value_add.append(dot_nn(terms.astype(BF16), gs[head, span(i, tile), :]))
                    key_add.append(dot_nn(slopes, qs[head, span(i, tile), :]))
                    rows = slice(head * HEAD_DIM, (head + 1) * HEAD_DIM)
                    dqt[i, rows, :] += dot_nn(kt[j, rows, :], slopes)
                dk[...] += key_add[0] + key_add[1]
                dv[...] += value_add[0] + value_add[1]

            query_tile(j, True)

            def later(i, carry):
                query_tile(i, False)
                return carry

            lax.fori_loop(j + 1, tiles, later, 0)
            dsort[1, span(j, tile), :] = dk[...].astype(BF16)
            dsort[2, span(j, tile), :] = dv[...].astype(BF16)
            sum_ref[1:2, :] += jnp.sum(dv[...], axis=0, keepdims=True)
            return carry

        lax.fori_loop(0, tiles, key_tile, 0)

        def finish(t, carry):
            query_grad = dqt[t].T * SCALE
            dsort[0, span(t, tile), :] = query_grad.astype(BF16)
            sum_ref[0:1, :] += jnp.sum(query_grad, axis=0, keepdims=True)
            return carry

        lax.fori_loop(0, tiles, finish, 0)

        for step, entries in enumerate(layout):
            base = 0
            for offset, other in entries:
                device = device_at(chips, spot_ref, offset, other)
                for part in range(4 if other is None else 2):
                    there = span(order_ref[2 * device + part], blk)
                    for kind in range(3):
                        d_refs[step][base : base + blk, kind * SLOT : (kind + 1) * SLOT] = dsort[kind, there, :]
                    base += blk

    outs = [shape_of(8, SLOT, F32)]
    for entries in layout:
        rows = sum(4 * blk if other is None else 2 * blk for _, other in entries)
        outs.append(shape_of(rows, 3 * SLOT, BF16))
    scratch = [
        pltpu.VMEM((2, seq, SLOT), BF16),
        pltpu.VMEM((seq, SLOT), F32),
        pltpu.VMEM((tiles, SLOT, tile), BF16),
        pltpu.VMEM((tiles, SLOT, tile), F32),
        pltpu.VMEM((tiles, 8, tile), F32),
        pltpu.VMEM((tile, SLOT), F32),
        pltpu.VMEM((tile, SLOT), F32),
        pltpu.VMEM((3, seq, SLOT), BF16),
    ]
    args = [order, spot, queries, keys, values, grads, mixed, lse]
    ins = [SMEM_SPEC] * 2 + [VMEM_SPEC] * 6
    result = local_call(
        kernel, "attend_backward", outs, ins, args, 10 * seq * seq * SLOT, scratch, seq * seq
    )
    return list(result[1:]), result[0]


def body(
    tokens,
    cotangent,
    block_order,
    ln1_gain,
    ln1_bias,
    w_qkv,
    qv_bias,
    w_out,
    out_bias,
    ln2_gain,
    ln2_bias,
    w_fc,
    fc_bias,
    w_proj,
    proj_bias,
):
    width = HEADS * HEAD_DIM
    half = width // 2
    count = lax.axis_size("context")
    rows = tokens.shape[1]
    seq = count * rows
    blk = rows // 2
    hidden = fc_bias.shape[0] * 2
    share = hidden // count
    own_rows = w_qkv.shape[0]
    padded = count * SLOT
    grad_scale = 1.0 / math.sqrt(lax.axis_size("fsdp") * seq)
    side = lax.axis_index("fsdp")
    ring = Ring(count)
    mine, layout, far = ring.mine, ring.layout(), ring.far
    upper = mine // (count // 2)
    order = block_order.astype(jnp.int32)
    spot = ring.spot
    sizes = [[2 * rows if other is None else rows for _, other in entries] for entries in layout]

    vectors = jnp.concatenate(
        [
            jnp.stack(
                [ln1_gain, ln1_bias, qv_bias[:, 0], qv_bias[:, 1], out_bias, ln2_gain, ln2_bias, proj_bias]
            ),
            fc_bias.reshape(-1, half),
        ],
        axis=0,
    )
    low, high = pair_halves(vectors, side)
    rows_of = jnp.concatenate([low[:8], high[:8]], axis=1).astype(F32)
    gain_one, shift_one, q_bias, v_bias, out_b, gain_two, shift_two, proj_b = [rows_of[i : i + 1] for i in range(8)]
    fc_b = jnp.concatenate([low[8:].reshape(-1), high[8:].reshape(-1)])
    fc_b = lax.dynamic_slice(fc_b, (mine * share,), (share,)).astype(F32)[None]
    slot_bias = jnp.concatenate([q_bias, jnp.zeros_like(q_bias), v_bias], axis=0)
    slot_bias = jnp.pad(slot_bias, ((0, 0), (0, padded - width)))
    slot_bias = lax.dynamic_slice(slot_bias, (0, mine * SLOT), (3, SLOT)).reshape(1, 3 * SLOT)

    xs16 = tokens[0]
    xs = xs16.astype(F32)
    head_blocks = start_heads(w_qkv, side, count)
    landed_heads = spread(head_blocks)
    w_heads = wide(finish_heads(landed_heads, side, own_rows, width), 0)
    x_steps, h_one, n_one = [], [], []

    def visit_tokens(step, blocks):
        h_blocks, n_blocks = norm_blocks(blocks, wide(gain_one), wide(shift_one), width)
        x_steps.append(blocks)
        h_one.append(h_blocks)
        n_one.append(n_blocks)
        return h_blocks[0]

    def hold_tokens(step, value):
        if step == 2:
            return after(value, head_blocks)
        return after(value, landed_heads) if step == far else value

    ring.gather(wide(xs16), visit_tokens, hold_tokens)

    low, high = pair_halves(w_out, side)
    w_out_rows = after(jnp.concatenate([low, high], axis=1), x_steps[far - 1][0])
    w_out_all = lax.all_gather(w_out_rows, "context", axis=0, tiled=True)
    fc_blocks = start_fc(after(w_fc, landed_heads), side, count, share)
    landed_fc = spread(fc_blocks)
    w_fc_part = wide(finish_fc(landed_fc, side, upper, own_rows), 0)
    cot16 = cotangent[0]
    cot_all = lax.all_gather(after(wide(cot16), x_steps[far][0]), "context", axis=0, tiled=True)
    low, high = pair_halves(after(w_proj, w_heads), side)
    w_proj_part = wide(jnp.concatenate([low, high], axis=1))

    mixed, lse, *saved = attend_forward(order, spot, h_one, after(w_heads, fc_blocks), slot_bias, layout, blk)
    mixed = after(mixed, landed_fc)
    attn_out = lax.all_to_all(mixed, "context", 0, 1, tiled=True)[:, :width]

    resid_one = xs + dot_nn(attn_out, w_out_all) + out_b
    normed_two, inv_two = norm_stats(resid_one)
    h_two = (normed_two * gain_two + shift_two).astype(BF16)

    h_steps, acts, slopes, bias_sums, h2_terms = [], [], [], [], []

    def visit_feed(step, blocks):
        act, slope, bias_sum, terms = feed_blocks(
            spot, blocks, cot_all, w_fc_part, w_proj_part, fc_b, ring.size, layout[step]
        )
        h_steps.append(blocks)
        acts.append(act)
        slopes.append(slope)
        bias_sums.append(bias_sum)
        h2_terms.append(terms)
        return bias_sum

    ring.gather(wide(h_two), visit_feed)
    h_two_all, acts_all, slopes_all = pack(spot, [h_steps, acts, slopes], layout, ring.size, seq)

    g_fc = (dot_tn(h_two_all, slopes_all)[:width] * grad_scale).astype(BF16)
    g_proj = dot_tn(acts_all, cot_all)[:, :width] * grad_scale
    fillers = {far - 1: g_fc, far - 2: g_proj}

    def hold_feed(step, value):
        return after(value, fillers[step]) if step in fillers else value

    grad_h2 = ring.scatter(lambda step, event: h2_terms[step], hold_feed)[:, :width]
    g_w_proj = pair_sum(g_proj[:, :half], g_proj[:, half:], side)

    grad_y = cot16.astype(F32)
    normed_one, inv_one = norm_stats(xs)
    grad_r1 = grad_y + norm_back(grad_h2, normed_two, inv_two, gain_two)
    grad_r16 = grad_r1.astype(BF16)
    grad_o16 = dot_nt(grad_r16, w_out_all).astype(BF16)
    grad_heads = lax.all_to_all(
        jnp.pad(grad_o16, ((0, 0), (0, padded - width))), "context", 1, 0, tiled=True
    )
    g_out = dot_tn(attn_out, grad_r16) * grad_scale
    g_out = pair_sum(g_out[:, :half], g_out[:, half:], side).astype(BF16).reshape(count, own_rows, half)

    def give_out(step, event):
        act = after(acts[step], grad_o16 if event is None else event)
        return project_blocks(act, w_proj_part, sizes[step])

    out_events = []

    def hold_out(step, value):
        out_events.append(value)
        return value

    result = (resid_one + ring.scatter(give_out, hold_out)[:, :width] + proj_b).astype(BF16)
    g_w_fc = return_fc(after(g_fc, grad_o16), side, upper, count, share, own_rows)

    grad_heads = after(grad_heads, out_events[0])
    d_steps, head_sums = attend_backward(order, spot, saved, grad_heads, mixed, lse, layout, blk)
    norm_sums = []

    def give_input(step, event):
        grad = d_steps[step] if event is None else after(d_steps[step], event)
        sums, terms = input_blocks(grad, w_heads, n_one[step])
        norm_sums.append(sums)
        return terms

    h_one_all, d_all = pack(spot, [h_one, d_steps], layout, ring.size, seq)
    g_qkv = (dot_tn(h_one_all, d_all)[:width] * grad_scale).astype(BF16)
    grad_h1 = ring.scatter(give_input, lambda step, value: after(value, g_qkv) if step == far - 2 else value)
    grad_h1 = grad_h1[:, :width]
    grad_x = (grad_r1 + norm_back(grad_h1, normed_one, inv_one, gain_one)).astype(BF16)
    g_w_qkv = return_heads(g_qkv, side, count, own_rows, width)

    even = even_rows(g_out, 1).reshape(ring.size, -1, half)
    g_w_out = ring.scatter(lambda step, event, blocks=ring.pick(even): blocks[step])[:own_rows]

    fc_place = lax.dynamic_update_slice(jnp.zeros((hidden,), F32), total(bias_sums)[0], (mine * share,))
    head_place = lax.dynamic_update_slice(
        jnp.zeros((2, padded), F32), head_sums[:2], (jnp.int32(0), mine * SLOT)
    )[:, :width]
    local = jnp.concatenate(
        [
            jnp.sum(grad_h2 * normed_two, axis=0),
            jnp.sum(grad_h2, axis=0),
            jnp.sum(grad_r1, axis=0),
            jnp.sum(grad_y, axis=0),
            fc_place,
            total(norm_sums)[:, :width].reshape(-1),
            head_place.reshape(-1),
        ]
    )
    sums = sum_everywhere(local.reshape(-1, SLOT) * grad_scale, count).reshape(-1)

    def own_half(vector):
        return lax.dynamic_slice(vector, (side * (vector.shape[0] // 2),), (vector.shape[0] // 2,))

    g_ln2_gain, g_ln2_bias, g_out_bias, g_proj_bias = [
        own_half(sums[i * width : (i + 1) * width]) for i in range(4)
    ]
    g_fc_bias = own_half(sums[4 * width : 4 * width + hidden])
    late = sums[4 * width + hidden :]
    g_ln1_gain, g_ln1_bias, g_q, g_v = [own_half(late[i * width : (i + 1) * width]) for i in range(4)]
    return (
        result[None],
        grad_x[None],
        g_ln1_gain,
        g_ln1_bias,
        g_w_qkv,
        jnp.stack([g_q, g_v], axis=1),
        g_w_out,
        g_out_bias,
        g_ln2_gain,
        g_ln2_bias,
        g_w_fc,
        g_fc_bias,
        g_w_proj,
        g_proj_bias,
    )


def solution(mesh):
    rows = P("fsdp", "context", None)
    weight = P("context", "fsdp")
    vector = P("fsdp")
    pair = P("fsdp", None)
    return jax.shard_map(
        body,
        mesh=mesh,
        in_specs=(
            rows, rows, P(), vector, vector, weight, pair, weight,
            vector, vector, vector, weight, vector, weight, vector,
        ),
        out_specs=(
            rows, rows, vector, vector, weight, pair, weight,
            vector, vector, vector, weight, vector, weight, vector,
        ),
        check_vma=False,
    )
```

```python
import functools
import math

import jax
import jax.numpy as jnp
from jax import lax
from jax.experimental import pallas as pl
from jax.experimental.pallas import tpu as pltpu
from jax.sharding import PartitionSpec as P

HEADS = 25
HEAD_DIM = 64
SLOT = 2 * HEAD_DIM

EPSILON = 1e-05
GELU_ROOT = math.sqrt(2.0 / math.pi)
GELU_CUBIC = 0.044715
NEG_LARGE = -1e30
SCALE = HEAD_DIM ** (-0.5)
VMEM_LIMIT = 56 * 1024 * 1024
F32 = jnp.float32
BF16 = jnp.bfloat16


def norm_stats(values):
    centred = values - jnp.mean(values, axis=-1, keepdims=True)
    inv_std = lax.rsqrt(jnp.mean(centred * centred, axis=-1, keepdims=True) + EPSILON)
    return centred * inv_std, inv_std


def norm_back(upstream, normed, inv_std, gain_vec):
    scaled = upstream * gain_vec
    return inv_std * (
        scaled
        - jnp.mean(scaled, axis=-1, keepdims=True)
        - normed * jnp.mean(scaled * normed, axis=-1, keepdims=True)
    )


def gelu_pair(pre_act):
    inner = GELU_ROOT * (pre_act + GELU_CUBIC * pre_act * pre_act * pre_act)
    tangent = jnp.tanh(inner)
    act_value = 0.5 * pre_act * (1.0 + tangent)
    act_slope = 0.5 * (1.0 + tangent) + 0.5 * pre_act * (1.0 - tangent * tangent) * GELU_ROOT * (
        1.0 + 3.0 * GELU_CUBIC * pre_act * pre_act
    )
    return (act_value, act_slope)


class Ring:
    def __init__(self, count):
        chips = count // 2
        self.count, self.size, self.far = count, chips, chips // 2
        self.mine = lax.axis_index("context")
        self.core = self.mine % 2
        chip = self.mine // 2
        if chips == 8:
            order = [0, 2, 4, 6, 7, 5, 3, 1]
            self.place = jnp.where(chip % 2 == 0, chip // 2, (15 - chip) // 2)
        else:
            order = list(range(chips))
            self.place = chip
        self.spot = jnp.stack([self.place, self.core]).astype(jnp.int32)
        self.links = []
        for i in range(chips):
            self.links.append((2 * order[i], 2 * order[(i + 1) % chips]))
            self.links.append((2 * order[i] + 1, 2 * order[(i - 1) % chips] + 1))
        self.swaps = [(i, i ^ 1) for i in range(count)]

    def layout(self):
        steps = [[(0, None)]] + [[(step, None), (-step, None)] for step in range(1, self.far)]
        return steps + [[(self.far, 0), (self.far, 1)]]

    def swap(self, value):
        return lax.ppermute(value, "context", self.swaps)

    def send(self, value):
        return lax.ppermute(value, "context", self.links)

    def own(self, value, other=0):
        rows = value.shape[0] // 2
        return lax.dynamic_slice_in_dim(value, (self.core ^ other) * rows, rows)

    def gather(self, block, visit, hold=None):
        other = self.swap(block)
        current = jnp.concatenate(
            [jnp.where(self.core == 0, block, other), jnp.where(self.core == 0, other, block)], axis=0
        )
        blocks = [current]
        for step in range(1, self.far + 1):
            if step == self.far:
                current = self.own(current)
            if hold is not None:
                current = hold(step, current)
            event = visit(step - 1, blocks)
            current = self.send(current)
            if event is not None:
                current = after(current, event)
            blocks = [current, self.swap(current)]
        visit(self.far, blocks)

    def pick(self, array):
        cut = array.shape[1] // 2
        steps = []
        for entries in self.layout():
            blocks = []
            for offset, other in entries:
                first, size = (0, 2 * cut) if other is None else ((self.core ^ other) * cut, cut)
                chip = device_at(self.size, self.spot, offset, None) // 2
                blocks.append(lax.dynamic_slice(array, (chip, first, 0), (1, size, array.shape[2]))[0])
            steps.append(blocks)
        return steps

    def scatter(self, give, fill=None):
        sent = None
        for step in range(self.far, 0, -1):
            first, second = give(step, sent)
            if step == self.far:
                value = total([first, self.swap(second)])
            else:
                value = total([second, self.swap(first)])
            if step == self.far - 1:
                got = got.astype(F32)
                blank = jnp.zeros_like(got)
                value = value + jnp.concatenate(
                    [jnp.where(self.core == 0, got, blank), jnp.where(self.core == 0, blank, got)], axis=0
                )
            elif step < self.far - 1:
                value = value + got.astype(F32)
            sent = value.astype(BF16)
            got = self.send(sent)
            events = fill(step, sent) if fill is not None else ()
            if events:
                got = after(got, *events)
        value = total([give(0, sent)[0], got])
        return self.own(value) + self.swap(self.own(value, 1).astype(BF16)).astype(F32)


def device_at(size, spot, offset, other):
    place, core = spot[0], spot[1]
    at = lax.rem(place + offset * (2 * core - 1) + size, size)
    chip = jnp.where(at < 4, 2 * at, 15 - 2 * at) if size == 8 else at
    return 2 * chip if other is None else 2 * chip + (core ^ other)


def wide(value, axis=-1):
    axis %= value.ndim
    more = -value.shape[axis] % 128
    return jnp.pad(value, [(0, more if i == axis else 0) for i in range(value.ndim)])


def total(values):
    result = values[0].astype(F32)
    for value in values[1:]:
        result = result + value.astype(F32)
    return result


def after(value, *events):
    return lax.optimization_barrier((value,) + events)[0]


def cross(value):
    return lax.ppermute(value, "fsdp", [(0, 1), (1, 0)])


def pair_halves(own, side):
    got = cross(own)
    return jnp.where(side == 0, own, got), jnp.where(side == 0, got, own)


def pair_sum(left, right, side):
    got = cross(jnp.where(side == 0, right, left).astype(BF16))
    return jnp.where(side == 0, left, right).astype(F32) + got.astype(F32)


def sum_everywhere(value, count):
    step = 1
    while step < count:
        value = value + lax.ppermute(value, "context", [(i, i ^ step) for i in range(count)])
        step *= 2
    return value + cross(value)


def even_rows(value, axis=0):
    odd = value.shape[axis] % 2
    if not odd:
        return value
    return jnp.pad(value, [(0, odd if i == axis else 0) for i in range(value.ndim)])


def spread(value):
    return lax.all_to_all(value, "context", 0, 0, tiled=True)


def start_fc(w_fc, side, count, share):
    w_fc = even_rows(w_fc)
    cut = w_fc.shape[0] // 2
    mine, got = w_fc[:cut], cross(w_fc[cut:])
    blocks = jnp.concatenate([jnp.where(side == 0, mine, got), jnp.where(side == 0, got, mine)], axis=1)
    return blocks.reshape(cut, count, share).transpose(1, 0, 2)


def finish_fc(landed, side, upper, rows):
    other = cross(landed)
    is_first = upper == side
    both = jnp.concatenate(
        [jnp.where(is_first, landed, other), jnp.where(is_first, other, landed)], axis=1
    )
    return both[:, :rows].reshape(landed.shape[0] * rows, landed.shape[2])


def return_fc(landed, side, count, rows):
    low, high = landed[: count // 2], landed[count // 2 :]
    mine, got = jnp.where(side == 0, low, high), cross(jnp.where(side == 0, high, low))
    both = jnp.concatenate([mine, got], axis=1).astype(F32).transpose(1, 0, 2)
    return both.reshape(both.shape[0], -1)[:rows]


def start_heads(w_qkv, side, count):
    rows, width = w_qkv.shape[0], w_qkv.shape[1] * 2 // 3
    half = width // 2
    main = jnp.where(side == 0, w_qkv[:, :width], w_qkv[:, half:])
    keys = even_rows(jnp.where(side == 0, w_qkv[:, width:], w_qkv[:, :half]))
    cut = keys.shape[0] // 2
    first, second = keys[:cut], keys[cut:]
    got = cross(jnp.where(side == 0, second, first))
    keys = jnp.concatenate([jnp.where(side == 0, first, got), jnp.where(side == 0, got, second)], axis=1)
    blocks = jnp.pad(jnp.concatenate([main, keys], axis=0), ((0, 0), (0, count * SLOT - width)))
    return blocks.reshape(rows + cut, count, SLOT).transpose(1, 0, 2)


def finish_heads(landed, other, side, rows, width):
    one, two = jnp.where(side == 0, landed, other), jnp.where(side == 0, other, landed)
    keys = jnp.concatenate([one[:, rows:], two[:, rows:]], axis=1)[:, :rows]
    heads = jnp.concatenate([one[:, :rows], keys, two[:, :rows]], axis=2)
    return heads.reshape(width, 3 * SLOT)


def return_heads(landed, side, count, rows, width):
    half = width // 2
    landed = landed.transpose(1, 0, 2).reshape(-1, count * SLOT)[:, :width]
    main, keys = landed[:rows], landed[rows:]
    low, high = keys[:, :half], keys[:, half:]
    got, own = cross(jnp.where(side == 0, high, low)), jnp.where(side == 0, low, high)
    keys = jnp.concatenate([jnp.where(side == 0, own, got), jnp.where(side == 0, got, own)], axis=0)[:rows]
    return jnp.where(
        side == 0, jnp.concatenate([main, keys], axis=1), jnp.concatenate([keys, main], axis=1)
    ).astype(F32)


def dot_nt(first, second):
    return lax.dot_general(first, second, (((1,), (1,)), ((), ())), preferred_element_type=F32)


def dot_nn(first, second):
    return lax.dot_general(first, second, (((1,), (0,)), ((), ())), preferred_element_type=F32)


def dot_tn(first, second):
    return lax.dot_general(first, second, (((0,), (0,)), ((), ())), preferred_element_type=F32)


VMEM_SPEC = pl.BlockSpec(memory_space=pltpu.VMEM)
SMEM_SPEC = pl.BlockSpec(memory_space=pltpu.SMEM)
ANY_SPEC = pl.BlockSpec(memory_space=pl.ANY)


def local_call(kernel, name, outs, ins, args, flops, scratch=(), exps=0):
    moved = sum(math.prod(x.shape) * x.dtype.itemsize for x in list(args) + list(outs))
    return pl.pallas_call(
        kernel,
        out_shape=tuple(outs),
        in_specs=list(ins),
        out_specs=tuple(VMEM_SPEC for _ in outs),
        scratch_shapes=list(scratch),
        compiler_params=pltpu.CompilerParams(vmem_limit_bytes=VMEM_LIMIT),
        cost_estimate=pl.CostEstimate(flops=flops, bytes_accessed=moved, transcendentals=exps),
        name=name,
    )(*args)


def shape_of(rows, cols, kind):
    return jax.ShapeDtypeStruct((rows, cols), kind)


def norm_blocks(blocks, gain, shift, width):
    count = len(blocks)

    def kernel(*refs):
        ins, gain_ref, shift_ref, outs = refs[:count], refs[count], refs[count + 1], refs[count + 2 :]
        for i in range(count):
            values = ins[i][...].astype(F32)
            lane = lax.broadcasted_iota(jnp.int32, (1, values.shape[1]), 1)
            centred = values - jnp.sum(values, axis=-1, keepdims=True) * (1.0 / width)
            centred = jnp.where(lane < width, centred, 0.0)
            spread_of = jnp.sum(centred * centred, axis=-1, keepdims=True) * (1.0 / width)
            normed = centred * lax.rsqrt(spread_of + EPSILON)
            outs[i][...] = (normed * gain_ref[...] + shift_ref[...]).astype(BF16)
            outs[count + i][...] = normed.astype(BF16)

    outs = [jax.ShapeDtypeStruct(x.shape, BF16) for x in blocks] * 2
    args = list(blocks) + [gain, shift]
    size = sum(x.size for x in blocks)
    result = local_call(kernel, "norm_blocks", outs, [VMEM_SPEC] * len(args), args, 10 * size)
    return list(result[:count]), list(result[count:])


def feed_blocks(blocks, cots, w_fc, w_proj, bias):
    count, (width, share) = len(blocks), w_fc.shape
    sizes = [x.shape[0] for x in blocks]
    rows = sum(sizes)

    def kernel(*refs):
        h_refs, c_refs = refs[:count], refs[count : 2 * count]
        fc_ref, proj_ref, bias_ref, act_ref, du_ref, sum_ref = refs[2 * count : 2 * count + 6]
        outs, results = refs[2 * count + 6 : 3 * count + 6], refs[3 * count + 6 :]
        rows_in = jnp.concatenate([ref[...] for ref in h_refs], axis=0)
        cot_in = jnp.concatenate([ref[...] for ref in c_refs], axis=0)
        act, slope = gelu_pair(dot_nn(rows_in, fc_ref[...]) + bias_ref[...])
        act_ref[...] = act.astype(BF16)
        grad = dot_nt(cot_in, proj_ref[...]) * slope
        sum_ref[...] = jnp.sum(grad, axis=0, keepdims=True)
        grad = grad.astype(BF16)
        du_ref[...] = grad
        terms = dot_nt(grad, fc_ref[...]).astype(BF16)
        output = dot_nn(act_ref[...], proj_ref[...]).astype(BF16)
        at = 0
        for i in range(count):
            outs[i][...] = terms[at : at + sizes[i]]
            results[i][...] = output[at : at + sizes[i]]
            at += sizes[i]

    outs = [shape_of(rows, share, BF16), shape_of(rows, share, BF16), shape_of(1, share, F32)]
    outs += [shape_of(size, width, BF16) for size in sizes] * 2
    args = list(blocks) + list(cots) + [w_fc, w_proj, bias]
    result = local_call(
        kernel, "feed_blocks", outs, [VMEM_SPEC] * len(args), args, 8 * rows * width * share, exps=rows * share
    )
    return result[0], result[1], result[2], list(result[3 : 3 + count]), list(result[3 + count :])


def input_blocks(grad, w_heads, normed):
    count, width = len(normed), w_heads.shape[0]
    sizes = [x.shape[0] for x in normed]

    def kernel(*refs):
        grad_ref, w_ref, n_refs, sum_ref, outs = refs[0], refs[1], refs[2 : 2 + count], refs[2 + count], refs[3 + count :]
        terms = dot_nt(grad_ref[...], w_ref[...])
        gains = jnp.zeros((1, width), F32)
        at = 0
        for i, size in enumerate(sizes):
            term = terms[at : at + size]
            at += size
            outs[i][...] = term.astype(BF16)
            gains += jnp.sum(term * n_refs[i][...].astype(F32), axis=0, keepdims=True)
        sum_ref[0:1, :] = gains
        sum_ref[1:2, :] = jnp.sum(terms, axis=0, keepdims=True)

    outs = [shape_of(2, width, F32)] + [shape_of(size, width, BF16) for size in sizes]
    args = [grad, w_heads] + list(normed)
    result = local_call(
        kernel, "input_blocks", outs, [VMEM_SPEC] * len(args), args, 2 * grad.size * width
    )
    return result[0], list(result[1:])


def weight_terms(flags, steps, grads, scale, count, rows, heads):
    flat = [block for blocks in steps for block in blocks]
    width, cols = flat[0].shape[1], grads[0].shape[1]
    cut = (rows + 1) // 2
    shape = (count, rows + cut, SLOT) if heads else (count, cut, cols)

    def kernel(*refs):
        flag_ref, h_refs = refs[0], refs[1 : 1 + len(flat)]
        g_refs, (keep_ref, send_ref, held, part) = refs[1 + len(flat) : -4], refs[-4:]
        product, index = None, 0
        for step, blocks in enumerate(steps):
            at = 0
            for block in blocks:
                size = block.shape[0]
                add = dot_tn(g_refs[step][at : at + size, :], h_refs[index][...])
                product = add if product is None else product + add
                at += size
                index += 1
        held[...] = product.T * scale

        def give(out_ref, second):
            for d in range(count):
                if heads:
                    lanes = slice(2 * SLOT, 3 * SLOT) if second else slice(0, SLOT)
                    part[0:rows, :] = held[d * rows : (d + 1) * rows, lanes]
                    first = d * rows + (cut if second else 0)
                    part[rows : rows + cut, :] = held[first : first + cut, SLOT : 2 * SLOT]
                    out_ref[d] = part[0 : rows + cut, :].astype(BF16)
                else:
                    first = d * rows + (cut if second else 0)
                    out_ref[d] = held[first : first + cut, :].astype(BF16)

        @pl.when(flag_ref[0] == 0)
        def _():
            give(keep_ref, False)
            give(send_ref, True)

        @pl.when(flag_ref[0] != 0)
        def _():
            give(keep_ref, True)
            give(send_ref, False)

    outs = [jax.ShapeDtypeStruct(shape, BF16)] * 2
    args = [flags] + flat + list(grads)
    ins = [SMEM_SPEC] + [VMEM_SPEC] * (len(args) - 1)
    scratch = [pltpu.VMEM((width, cols), F32), pltpu.VMEM((rows + cut + 8, SLOT), F32)]
    total_rows = sum(x.shape[0] for x in flat)
    return local_call(kernel, "weight_terms", outs, ins, args, 2 * total_rows * width * cols, scratch)


def proj_terms(acts, steps, scale):
    flat = [block for blocks in steps for block in blocks]
    width, share = flat[0].shape[1], acts[0].shape[1]

    def kernel(*refs):
        c_refs, a_refs, out_ref = refs[: len(flat)], refs[len(flat) : -1], refs[-1]
        product, index = None, 0
        for step, blocks in enumerate(steps):
            at = 0
            for block in blocks:
                size = block.shape[0]
                add = dot_tn(a_refs[step][at : at + size, :], c_refs[index][...])
                product = add if product is None else product + add
                at += size
                index += 1
        out_ref[...] = product * scale

    outs = [shape_of(share, width, F32)]
    args = flat + list(acts)
    total_rows = sum(x.shape[0] for x in flat)
    flops = 2 * total_rows * width * share
    return local_call(kernel, "proj_terms", outs, [VMEM_SPEC] * len(args), args, flops)[0]


def out_blocks(spot, mixed, grad, layout, size, scale):
    (rows, height), cols = mixed.shape, grad.shape[1]
    unit = height // (2 * size)
    plan = [entry for entries in layout for entry in entries]

    def kernel(spot_ref, o_ref, grad_ref, *refs):
        outs, held = refs[:-1], refs[-1]
        turned = o_ref[...].astype(F32).T.astype(BF16)
        held[...] = dot_nn(turned, grad_ref[...]) * scale
        for i, (offset, other) in enumerate(plan):
            device = device_at(size, spot_ref, offset, other)
            block = held[pl.ds(pl.multiple_of(device * unit, 8), outs[i].shape[0]), :]
            outs[i][...] = block.astype(BF16)

    outs = [shape_of(2 * unit if other is None else unit, cols, BF16) for _, other in plan]
    result = local_call(
        kernel,
        "out_blocks",
        outs,
        [SMEM_SPEC] + [VMEM_SPEC] * 2,
        [spot, mixed, grad],
        2 * rows * height * cols,
        [pltpu.VMEM((height, cols), F32)],
    )
    steps, at = [], 0
    for entries in layout:
        steps.append(list(result[at : at + len(entries)]))
        at += len(entries)
    return steps


def head_masks(scale):
    lane = lax.broadcasted_iota(jnp.int32, (1, SLOT), 1)
    return [jnp.where(lane < HEAD_DIM, scale, 0.0), jnp.where(lane < HEAD_DIM, 0.0, scale)]


def flipped(value):
    return value.astype(F32).T


def causal(tile):
    keys = lax.broadcasted_iota(jnp.int32, (tile, tile), 0)
    queries = lax.broadcasted_iota(jnp.int32, (tile, tile), 1)
    return keys <= queries


def span(index, size):
    return pl.ds(pl.multiple_of(index * size, size), size)


def tile_of(seq):
    return math.gcd(seq, 512)


def attend_forward(order, spot, blocks, w_heads, bias, layout, blk):
    size = len(layout) - 1
    chips = 2 * size
    seq = 4 * chips * blk
    width = w_heads.shape[0]
    tile = tile_of(seq)
    tiles = seq // tile
    flat = [(step, entry) for step, entries in enumerate(layout) for entry in entries]
    pieces = len(flat)

    def kernel(*refs):
        order_ref, spot_ref = refs[:2]
        h_refs = refs[2 : 2 + pieces]
        w_ref, bias_ref, o_ref, lse_ref, qs, ks, vs, held, vt, os, sems = refs[2 + pieces :]
        masks = head_masks(SCALE)
        copies, starts, at = [], [], 0
        for i in range(pieces):
            rows = h_refs[i].shape[0]
            copy = pltpu.make_async_copy(h_refs[i], held.at[pl.ds(at, rows), :], sems.at[i])
            copy.start()
            copies.append(copy)
            starts.append(at)
            at += rows

        index = 0
        for step, entries in enumerate(layout):
            first = starts[index]
            for i in range(len(entries)):
                copies[index + i].wait()
            rows = sum(h_refs[index + i].shape[0] for i in range(len(entries)))
            mixed = dot_nn(held[first : first + rows, :], w_ref[...]) + bias_ref[...]
            for i, (offset, other) in enumerate(entries):
                base = starts[index + i] - first
                device = device_at(chips, spot_ref, offset, other)
                for part in range(4 if other is None else 2):
                    there = span(order_ref[2 * device + part], blk)
                    block = mixed[base : base + blk].astype(BF16)
                    base += blk
                    query = block[:, :SLOT].astype(F32)
                    for head in range(2):
                        qs[head, there, :] = (query * masks[head]).astype(BF16)
                    ks[there, :] = block[:, SLOT : 2 * SLOT]
                    vs[there, :] = block[:, 2 * SLOT :]
            index += len(entries)

        def turn(t, carry):
            vt[t] = flipped(vs[span(t, tile), :]).astype(BF16)
            return carry

        lax.fori_loop(0, tiles, turn, 0)
        visible = causal(tile)

        def query_tile(i, carry):
            def key_tile(j, state, diagonal):
                fresh = []
                for head in range(2):
                    top, sums, accum = state[3 * head : 3 * head + 3]
                    scores = dot_nt(ks[span(j, tile), :], qs[head, span(i, tile), :])
                    if diagonal:
                        scores = jnp.where(visible, scores, NEG_LARGE)
                    new_top = jnp.maximum(top, jnp.max(scores, axis=0, keepdims=True))
                    terms = jnp.exp(scores - new_top)
                    decay = jnp.exp(top - new_top)
                    sums = sums * decay + jnp.sum(terms, axis=0, keepdims=True)
                    values = vt[j, head * HEAD_DIM : (head + 1) * HEAD_DIM, :]
                    accum = accum * decay + dot_nn(values, terms.astype(BF16))
                    fresh += [new_top, sums, accum]
                return tuple(fresh)

            start = (
                jnp.full((1, tile), NEG_LARGE, F32),
                jnp.zeros((1, tile), F32),
                jnp.zeros((HEAD_DIM, tile), F32),
            )
            state = lax.fori_loop(0, i, lambda j, state: key_tile(j, state, False), start + start)
            state = key_tile(i, state, True)
            mixed = jnp.concatenate([state[2] / state[1], state[5] / state[4]], axis=0)
            os[span(i, tile), :] = mixed.T.astype(BF16)
            for head in range(2):
                lse_ref[i, head : head + 1, :] = state[3 * head] + jnp.log(state[3 * head + 1])
            return carry

        lax.fori_loop(0, tiles, query_tile, 0)

        def sort_out(s, carry):
            o_ref[span(s, blk), :] = os[span(order_ref[s], blk), :]
            return carry

        lax.fori_loop(0, seq // blk, sort_out, 0)

    outs = [
        shape_of(seq, SLOT, BF16),
        jax.ShapeDtypeStruct((tiles, 8, tile), F32),
        jax.ShapeDtypeStruct((2, seq, SLOT), BF16),
        shape_of(seq, SLOT, BF16),
        shape_of(seq, SLOT, BF16),
    ]
    scratch = [
        pltpu.VMEM((seq, width), BF16),
        pltpu.VMEM((tiles, SLOT, tile), BF16),
        pltpu.VMEM((seq, SLOT), BF16),
        pltpu.SemaphoreType.DMA((pieces,)),
    ]
    args = [order, spot] + [block for step in blocks for block in step] + [w_heads, bias]
    ins = [SMEM_SPEC] * 2 + [ANY_SPEC] * pieces + [VMEM_SPEC] * 2
    flops = 4 * seq * seq * SLOT + 6 * seq * width * SLOT
    return local_call(kernel, "attend_forward", outs, ins, args, flops, scratch, seq * seq)


def attend_backward(order, spot, saved, grads, mixed, lse, layout, blk):
    queries, keys, values = saved
    seq = keys.shape[0]
    chips = 2 * (len(layout) - 1)
    tile = tile_of(seq)
    tiles = seq // tile
    steps = len(layout)

    def kernel(order_ref, spot_ref, qs, ks, vs, g_ref, o_ref, lse_ref, sum_ref, *refs):
        d_refs = refs[:steps]
        gs, ps, kt, dqt, drow, dk, dv, dsort = refs[steps:]
        g_masks = head_masks(1.0)

        def sort_in(s, carry):
            here, there = span(s, blk), span(order_ref[s], blk)
            g_block = g_ref[here, :].astype(F32)
            for head in range(2):
                gs[head, there, :] = (g_block * g_masks[head]).astype(BF16)
            ps[there, :] = g_block * o_ref[here, :].astype(F32)
            return carry

        lax.fori_loop(0, seq // blk, sort_in, 0)

        def turn(t, carry):
            kt[t] = flipped(ks[span(t, tile), :]).astype(BF16)
            products = ps[span(t, tile), :].T
            for head in range(2):
                drow[t, head : head + 1, :] = jnp.sum(
                    products[head * HEAD_DIM : (head + 1) * HEAD_DIM], axis=0, keepdims=True
                )
            dqt[t] = jnp.zeros((SLOT, tile), F32)
            return carry

        lax.fori_loop(0, tiles, turn, 0)
        visible = causal(tile)
        sum_ref[...] = jnp.zeros(sum_ref.shape, F32)

        def key_tile(j, carry):
            dk[...] = jnp.zeros(dk.shape, F32)
            dv[...] = jnp.zeros(dv.shape, F32)

            def query_tile(i, diagonal):
                key_add, value_add = [], []
                for head in range(2):
                    scores = dot_nt(ks[span(j, tile), :], qs[head, span(i, tile), :])
                    terms = jnp.exp(scores - lse_ref[i, head : head + 1, :])
                    if diagonal:
                        terms = jnp.where(visible, terms, 0.0)
                    slopes = dot_nt(vs[span(j, tile), :], gs[head, span(i, tile), :])
                    slopes = (terms * (slopes - drow[i, head : head + 1, :])).astype(BF16)
                    value_add.append(dot_nn(terms.astype(BF16), gs[head, span(i, tile), :]))
                    key_add.append(dot_nn(slopes, qs[head, span(i, tile), :]))
                    rows = slice(head * HEAD_DIM, (head + 1) * HEAD_DIM)
                    dqt[i, rows, :] += dot_nn(kt[j, rows, :], slopes)
                dk[...] += key_add[0] + key_add[1]
                dv[...] += value_add[0] + value_add[1]

            query_tile(j, True)

            def later(i, carry):
                query_tile(i, False)
                return carry

            lax.fori_loop(j + 1, tiles, later, 0)
            dsort[1, span(j, tile), :] = dk[...].astype(BF16)
            dsort[2, span(j, tile), :] = dv[...].astype(BF16)
            sum_ref[1:2, :] += jnp.sum(dv[...], axis=0, keepdims=True)
            return carry

        lax.fori_loop(0, tiles, key_tile, 0)

        def finish(t, carry):
            query_grad = dqt[t].T * SCALE
            dsort[0, span(t, tile), :] = query_grad.astype(BF16)
            sum_ref[0:1, :] += jnp.sum(query_grad, axis=0, keepdims=True)
            return carry

        lax.fori_loop(0, tiles, finish, 0)

        for step, entries in enumerate(layout):
            base = 0
            for offset, other in entries:
                device = device_at(chips, spot_ref, offset, other)
                for part in range(4 if other is None else 2):
                    there = span(order_ref[2 * device + part], blk)
                    for kind in range(3):
                        d_refs[step][base : base + blk, kind * SLOT : (kind + 1) * SLOT] = dsort[kind, there, :]
                    base += blk

    outs = [shape_of(8, SLOT, F32)]
    for entries in layout:
        rows = sum(4 * blk if other is None else 2 * blk for _, other in entries)
        outs.append(shape_of(rows, 3 * SLOT, BF16))
    scratch = [
        pltpu.VMEM((2, seq, SLOT), BF16),
        pltpu.VMEM((seq, SLOT), F32),
        pltpu.VMEM((tiles, SLOT, tile), BF16),
        pltpu.VMEM((tiles, SLOT, tile), F32),
        pltpu.VMEM((tiles, 8, tile), F32),
        pltpu.VMEM((tile, SLOT), F32),
        pltpu.VMEM((tile, SLOT), F32),
        pltpu.VMEM((3, seq, SLOT), BF16),
    ]
    args = [order, spot, queries, keys, values, grads, mixed, lse]
    ins = [SMEM_SPEC] * 2 + [VMEM_SPEC] * 6
    result = local_call(
        kernel, "attend_backward", outs, ins, args, 10 * seq * seq * SLOT, scratch, seq * seq
    )
    return list(result[1:]), result[0]


def body(
    tokens,
    cotangent,
    block_order,
    ln1_gain,
    ln1_bias,
    w_qkv,
    qv_bias,
    w_out,
    out_bias,
    ln2_gain,
    ln2_bias,
    w_fc,
    fc_bias,
    w_proj,
    proj_bias,
):
    width = HEADS * HEAD_DIM
    half = width // 2
    count = lax.axis_size("context")
    rows = tokens.shape[1]
    seq = count * rows
    blk = rows // 2
    hidden = fc_bias.shape[0] * 2
    share = hidden // count
    own_rows = w_qkv.shape[0]
    padded = count * SLOT
    grad_scale = 1.0 / math.sqrt(lax.axis_size("fsdp") * seq)
    side = lax.axis_index("fsdp")
    ring = Ring(count)
    mine, layout, far = ring.mine, ring.layout(), ring.far
    upper = mine // (count // 2)
    order = block_order.astype(jnp.int32)
    spot = ring.spot
    sizes = [[2 * rows if other is None else rows for _, other in entries] for entries in layout]

    vectors = jnp.concatenate(
        [
            jnp.stack(
                [ln1_gain, ln1_bias, qv_bias[:, 0], qv_bias[:, 1], out_bias, ln2_gain, ln2_bias, proj_bias]
            ),
            fc_bias.reshape(-1, half),
        ],
        axis=0,
    )
    low, high = pair_halves(vectors, side)
    rows_of = jnp.concatenate([low[:8], high[:8]], axis=1).astype(F32)
    gain_one, shift_one, q_bias, v_bias, out_b, gain_two, shift_two, proj_b = [rows_of[i : i + 1] for i in range(8)]
    fc_b = jnp.concatenate([low[8:].reshape(-1), high[8:].reshape(-1)])
    fc_b = lax.dynamic_slice(fc_b, (mine * share,), (share,)).astype(F32)[None]
    slot_bias = jnp.concatenate([q_bias, jnp.zeros_like(q_bias), v_bias], axis=0)
    slot_bias = jnp.pad(slot_bias, ((0, 0), (0, padded - width)))
    slot_bias = lax.dynamic_slice(slot_bias, (0, mine * SLOT), (3, SLOT)).reshape(1, 3 * SLOT)

    xs16 = tokens[0]
    xs = xs16.astype(F32)
    head_blocks = start_heads(w_qkv, side, count)
    landed_heads = spread(head_blocks)
    other_heads = cross(landed_heads)
    w_heads = wide(finish_heads(landed_heads, other_heads, side, own_rows, width), 0)
    x_steps, h_one, n_one = [], [], []

    def visit_tokens(step, blocks):
        h_blocks, n_blocks = norm_blocks(blocks, wide(gain_one), wide(shift_one), width)
        x_steps.append(blocks)
        h_one.append(h_blocks)
        n_one.append(n_blocks)
        return h_blocks[0]

    cot16 = cotangent[0]
    cot_wide = wide(cot16)

    low, high = pair_halves(w_out, side)
    w_out_rows = jnp.concatenate([low, high], axis=1)
    w_out_rows = jnp.pad(w_out_rows, ((0, -own_rows % 8), (0, 0)))
    out_rows = w_out_rows.shape[0]
    fc_blocks = start_fc(w_fc, side, count, share)
    made = {}

    def hold_tokens(step, value):
        if step == 1:
            value = after(value, w_out_rows)
        if step == 2:
            value = after(value, head_blocks)
        if step == 3:
            value = after(value, landed_heads)
        if step == far:
            value = after(value, fc_blocks, other_heads)
        made["tokens"] = value
        return value

    ring.gather(wide(xs16), visit_tokens, hold_tokens)

    w_out_all = lax.all_gather(after(w_out_rows, made["tokens"]), "context", axis=0, tiled=True)
    landed_fc = spread(after(fc_blocks, x_steps[far - 1][0]))
    low, high = pair_halves(after(w_proj, w_heads), side)
    w_proj_part = wide(jnp.concatenate([low, high], axis=1))

    mixed, lse, *saved = attend_forward(order, spot, h_one, w_heads, slot_bias, layout, blk)

    cot_steps = []
    ring.gather(
        cot_wide,
        lambda step, blocks: cot_steps.append(blocks),
        lambda step, value: after(value, made["tokens"] if step == 1 else mixed) if step <= 2 else value,
    )

    w_fc_part = wide(finish_fc(after(landed_fc, mixed), side, upper, own_rows), 0)
    mixed = after(mixed, landed_fc, w_proj_part, cot_steps[max(1, far // 4)][0])
    attn_out = lax.all_to_all(mixed, "context", 0, 1, tiled=True)[:, :width]
    attn_out = after(attn_out, w_fc_part, cot_steps[max(2, 3 * far // 4)][0]).reshape(rows, count, own_rows)
    attn_out = jnp.pad(attn_out, ((0, 0), (0, 0), (0, out_rows - own_rows))).reshape(rows, -1)

    resid_one = xs + dot_nn(attn_out, w_out_all) + out_b
    normed_two, inv_two = norm_stats(resid_one)
    h_two = (normed_two * gain_two + shift_two).astype(BF16)

    h_steps, acts, slopes, bias_sums, h2_terms, out_terms = [], [], [], [], [], []

    def visit_feed(step, blocks):
        act, slope, bias_sum, terms, outputs = feed_blocks(
            blocks, cot_steps[step], w_fc_part, w_proj_part, fc_b
        )
        h_steps.append(blocks)
        acts.append(act)
        slopes.append(slope)
        bias_sums.append(bias_sum)
        h2_terms.append(terms)
        out_terms.append(outputs)
        return bias_sum

    ring.gather(wide(h_two), visit_feed)

    is_first = (upper == side).astype(jnp.int32)

    def fill_feed(step, event):
        if step == far:
            flags = after(1 - is_first, event).reshape(1)
            made["fc"] = weight_terms(flags, h_steps, slopes, grad_scale, count, own_rows, False)
            made["fc_got"] = cross(made["fc"][1])
            return (made["fc"][1],)
        if step == far - 1:
            made["proj"] = proj_terms([after(acts[0], event)] + acts[1:], cot_steps, grad_scale)
            return (made["proj"],)
        if step == far - 2:
            g_proj = after(made["proj"], event)[:, :width]
            left, right = g_proj[:, :half], g_proj[:, half:]
            made["proj_keep"] = jnp.where(side == 0, left, right)
            send = jnp.where(side == 0, right, left).astype(BF16)
            made["proj_got"] = cross(send)
            made["fc_sum"] = total([after(made["fc"][0], event), made["fc_got"]]).astype(BF16)
            return (send, made["fc_sum"])
        return ()

    grad_h2 = ring.scatter(lambda step, event: h2_terms[step], fill_feed)[:, :width]

    grad_y = cot16.astype(F32)
    normed_one, inv_one = norm_stats(xs)
    grad_r1 = grad_y + norm_back(grad_h2, normed_two, inv_two, gain_two)
    grad_r16 = grad_r1.astype(BF16)
    grad_o16 = dot_nt(grad_r16, w_out_all).astype(BF16)
    grad_o16 = grad_o16.reshape(rows, count, out_rows)[:, :, :own_rows].reshape(rows, width)
    grad_slots = jnp.pad(grad_o16, ((0, 0), (0, padded - width)))
    grad_heads = lax.all_to_all(grad_slots, "context", 1, 0, tiled=True)

    g_out_steps = out_blocks(spot, after(attn_out, grad_slots), wide(grad_r16), layout, ring.size, grad_scale)
    g_out_events = {}

    def fill_out_grad(step, event):
        g_out_events[step] = event
        return ()

    g_out = ring.scatter(lambda step, event: g_out_steps[step], fill_out_grad)[:own_rows]
    g_w_out = pair_sum(g_out[:, :half], g_out[:, half:width], side)

    out_events = {}

    def give_out(step, event):
        return [after(term, grad_o16) for term in out_terms[step]] if event is None else out_terms[step]

    def fill_out(step, event):
        out_events[step] = event
        return ()

    result = (resid_one + ring.scatter(give_out, fill_out)[:, :width] + proj_b).astype(BF16)

    fc_sum = made["fc_sum"]
    fc_landed = spread(after(fc_sum, grad_heads))
    grad_heads = after(grad_heads, out_events[far - 1], g_out_events[far])
    d_steps, head_sums = attend_backward(order, spot, saved, grad_heads, mixed, lse, layout, blk)
    norm_sums = []

    def give_input(step, event):
        event = made[2] if step == 0 else event
        grad = d_steps[step] if event is None else after(d_steps[step], event)
        sums, terms = input_blocks(grad, w_heads, n_one[step])
        norm_sums.append(sums)
        return terms

    def fill_input(step, event):
        made[step] = event
        if step == far:
            flags = after(side, event).astype(jnp.int32).reshape(1)
            made["qkv"] = weight_terms(flags, h_one, d_steps, grad_scale, count, own_rows, True)
            return (made["qkv"][1], fc_landed)
        return ()

    grad_h1 = ring.scatter(give_input, fill_input)[:, :width]
    grad_x = (grad_r1 + norm_back(grad_h1, normed_one, inv_one, gain_one)).astype(BF16)
    keep, send = made["qkv"]
    qkv_sum = total([after(keep, made[far - 1]), cross(send)]).astype(BF16)
    g_w_qkv = return_heads(spread(qkv_sum), side, count, own_rows, width)
    g_w_proj = total([after(made["proj_keep"], made[2]), made["proj_got"]])
    g_w_fc = return_fc(after(fc_landed, made[2]), side, count, own_rows)

    fc_place = lax.dynamic_update_slice(jnp.zeros((hidden,), F32), total(bias_sums)[0], (mine * share,))
    head_place = lax.dynamic_update_slice(
        jnp.zeros((2, padded), F32), head_sums[:2], (jnp.int32(0), mine * SLOT)
    )[:, :width]
    local = jnp.concatenate(
        [
            jnp.sum(grad_h2 * normed_two, axis=0),
            jnp.sum(grad_h2, axis=0),
            jnp.sum(grad_r1, axis=0),
            jnp.sum(grad_y, axis=0),
            fc_place,
            total(norm_sums)[:, :width].reshape(-1),
            head_place.reshape(-1),
        ]
    )
    sums = sum_everywhere(local.reshape(-1, SLOT) * grad_scale, count).reshape(-1)

    def own_half(vector):
        return lax.dynamic_slice(vector, (side * (vector.shape[0] // 2),), (vector.shape[0] // 2,))

    g_ln2_gain, g_ln2_bias, g_out_bias, g_proj_bias = [
        own_half(sums[i * width : (i + 1) * width]) for i in range(4)
    ]
    g_fc_bias = own_half(sums[4 * width : 4 * width + hidden])
    late = sums[4 * width + hidden :]
    g_ln1_gain, g_ln1_bias, g_q, g_v = [own_half(late[i * width : (i + 1) * width]) for i in range(4)]
    return (
        result[None],
        grad_x[None],
        g_ln1_gain,
        g_ln1_bias,
        g_w_qkv,
        jnp.stack([g_q, g_v], axis=1),
        g_w_out,
        g_out_bias,
        g_ln2_gain,
        g_ln2_bias,
        g_w_fc,
        g_fc_bias,
        g_w_proj,
        g_proj_bias,
    )


def solution(mesh):
    rows = P("fsdp", "context", None)
    weight = P("context", "fsdp")
    vector = P("fsdp")
    pair = P("fsdp", None)
    return jax.shard_map(
        body,
        mesh=mesh,
        in_specs=(
            rows, rows, P(), vector, vector, weight, pair, weight,
            vector, vector, vector, weight, vector, weight, vector,
        ),
        out_specs=(
            rows, rows, vector, vector, weight, pair, weight,
            vector, vector, vector, weight, vector, weight, vector,
        ),
        check_vma=False,
    )
```

```python
import functools
import math

import jax
import jax.numpy as jnp
from jax import lax
from jax.experimental import pallas as pl
from jax.experimental.pallas import tpu as pltpu
from jax.sharding import PartitionSpec as P

HEADS = 25
HEAD_DIM = 64
SLOT = 2 * HEAD_DIM

EPSILON = 1e-05
GELU_ROOT = math.sqrt(2.0 / math.pi)
GELU_CUBIC = 0.044715
NEG_LARGE = -1e30
SCALE = HEAD_DIM ** (-0.5)
VMEM_LIMIT = 56 * 1024 * 1024
F32 = jnp.float32
BF16 = jnp.bfloat16


def norm_stats(values):
    centred = values - jnp.mean(values, axis=-1, keepdims=True)
    inv_std = lax.rsqrt(jnp.mean(centred * centred, axis=-1, keepdims=True) + EPSILON)
    return centred * inv_std, inv_std


def norm_back(upstream, normed, inv_std, gain_vec):
    scaled = upstream * gain_vec
    return inv_std * (
        scaled
        - jnp.mean(scaled, axis=-1, keepdims=True)
        - normed * jnp.mean(scaled * normed, axis=-1, keepdims=True)
    )


def gelu_pair(pre_act):
    inner = GELU_ROOT * (pre_act + GELU_CUBIC * pre_act * pre_act * pre_act)
    tangent = jnp.tanh(inner)
    act_value = 0.5 * pre_act * (1.0 + tangent)
    act_slope = 0.5 * (1.0 + tangent) + 0.5 * pre_act * (1.0 - tangent * tangent) * GELU_ROOT * (
        1.0 + 3.0 * GELU_CUBIC * pre_act * pre_act
    )
    return (act_value, act_slope)


class Ring:
    def __init__(self, count):
        chips = count // 2
        self.count, self.size, self.far = count, chips, chips // 2
        self.mine = lax.axis_index("context")
        self.core = self.mine % 2
        chip = self.mine // 2
        if chips == 8:
            order = [0, 2, 4, 6, 7, 5, 3, 1]
            self.place = jnp.where(chip % 2 == 0, chip // 2, (15 - chip) // 2)
        else:
            order = list(range(chips))
            self.place = chip
        self.spot = jnp.stack([self.place, self.core]).astype(jnp.int32)
        self.links = []
        for i in range(chips):
            self.links.append((2 * order[i], 2 * order[(i + 1) % chips]))
            self.links.append((2 * order[i] + 1, 2 * order[(i - 1) % chips] + 1))
        self.swaps = [(i, i ^ 1) for i in range(count)]

    def layout(self):
        steps = [[(0, None)]] + [[(step, None), (-step, None)] for step in range(1, self.far)]
        return steps + [[(self.far, 0), (self.far, 1)]]

    def swap(self, value):
        return lax.ppermute(value, "context", self.swaps)

    def send(self, value):
        return lax.ppermute(value, "context", self.links)

    def own(self, value, other=0):
        rows = value.shape[0] // 2
        return lax.dynamic_slice_in_dim(value, (self.core ^ other) * rows, rows)

    def gather(self, block, visit, hold=None):
        other = self.swap(block)
        current = jnp.concatenate(
            [jnp.where(self.core == 0, block, other), jnp.where(self.core == 0, other, block)], axis=0
        )
        blocks = [current]
        for step in range(1, self.far + 1):
            if step == self.far:
                current = self.own(current)
            if hold is not None:
                current = hold(step, current)
            event = visit(step - 1, blocks)
            current = self.send(current)
            if event is not None:
                current = after(current, event)
            blocks = [current, self.swap(current)]
        visit(self.far, blocks)

    def pick(self, array):
        cut = array.shape[1] // 2
        steps = []
        for entries in self.layout():
            blocks = []
            for offset, other in entries:
                first, size = (0, 2 * cut) if other is None else ((self.core ^ other) * cut, cut)
                chip = device_at(self.size, self.spot, offset, None) // 2
                blocks.append(lax.dynamic_slice(array, (chip, first, 0), (1, size, array.shape[2]))[0])
            steps.append(blocks)
        return steps

    def scatter(self, give, fill=None):
        going = Scatter(self, give)
        for step in range(self.far, 0, -1):
            going.hop()
            events = fill(step, going.sent) if fill is not None else ()
            going.hold(*events)
        return going.finish()


class Scatter:
    def __init__(self, ring, give):
        self.ring, self.give, self.step = ring, give, ring.far
        self.sent = self.got = None

    def hop(self, *events):
        ring, step = self.ring, self.step
        first, second = self.give(step, self.sent)
        if events:
            first, second = after(first, *events), after(second, *events)
        if step == ring.far:
            value = total([first, ring.swap(second)])
        else:
            value = total([second, ring.swap(first)])
        if step == ring.far - 1:
            got = self.got.astype(F32)
            blank = jnp.zeros_like(got)
            value = value + jnp.concatenate(
                [jnp.where(ring.core == 0, got, blank), jnp.where(ring.core == 0, blank, got)], axis=0
            )
        elif step < ring.far - 1:
            value = value + self.got.astype(F32)
        self.sent = value.astype(BF16)
        self.got = ring.send(self.sent)
        self.step -= 1

    def hold(self, *events):
        if events:
            self.got = after(self.got, *events)

    def finish(self):
        ring = self.ring
        while self.step:
            self.hop()
        value = total([self.give(0, self.sent)[0], self.got])
        return ring.own(value) + ring.swap(ring.own(value, 1).astype(BF16)).astype(F32)


def device_at(size, spot, offset, other):
    place, core = spot[0], spot[1]
    at = lax.rem(place + offset * (2 * core - 1) + size, size)
    chip = jnp.where(at < 4, 2 * at, 15 - 2 * at) if size == 8 else at
    return 2 * chip if other is None else 2 * chip + (core ^ other)


def wide(value, axis=-1):
    axis %= value.ndim
    more = -value.shape[axis] % 128
    return jnp.pad(value, [(0, more if i == axis else 0) for i in range(value.ndim)])


def total(values):
    result = values[0].astype(F32)
    for value in values[1:]:
        result = result + value.astype(F32)
    return result


def after(value, *events):
    return lax.optimization_barrier((value,) + events)[0]


def cross(value):
    return lax.ppermute(value, "fsdp", [(0, 1), (1, 0)])


def pair_halves(own, side):
    got = cross(own)
    return jnp.where(side == 0, own, got), jnp.where(side == 0, got, own)


def pair_sum(left, right, side):
    got = cross(jnp.where(side == 0, right, left).astype(BF16))
    return jnp.where(side == 0, left, right).astype(F32) + got.astype(F32)


def sum_everywhere(value, count):
    step = 1
    while step < count:
        value = value + lax.ppermute(value, "context", [(i, i ^ step) for i in range(count)])
        step *= 2
    return value + cross(value)


def even_rows(value, axis=0):
    odd = value.shape[axis] % 2
    if not odd:
        return value
    return jnp.pad(value, [(0, odd if i == axis else 0) for i in range(value.ndim)])


def spread(value):
    return lax.all_to_all(value, "context", 0, 0, tiled=True)


def start_fc(w_fc, side, count, share):
    w_fc = even_rows(w_fc)
    cut = w_fc.shape[0] // 2
    mine, got = w_fc[:cut], cross(w_fc[cut:])
    blocks = jnp.concatenate([jnp.where(side == 0, mine, got), jnp.where(side == 0, got, mine)], axis=1)
    return blocks.reshape(cut, count, share).transpose(1, 0, 2)


def finish_fc(landed, side, upper, rows):
    other = cross(landed)
    is_first = upper == side
    both = jnp.concatenate(
        [jnp.where(is_first, landed, other), jnp.where(is_first, other, landed)], axis=1
    )
    return both[:, :rows].reshape(landed.shape[0] * rows, landed.shape[2])


def return_fc(landed, side, count, rows):
    low, high = landed[: count // 2], landed[count // 2 :]
    mine, got = jnp.where(side == 0, low, high), cross(jnp.where(side == 0, high, low))
    both = jnp.concatenate([mine, got], axis=1).astype(F32).transpose(1, 0, 2)
    return both.reshape(both.shape[0], -1)[:rows]


def start_heads(w_qkv, side, count):
    rows, width = w_qkv.shape[0], w_qkv.shape[1] * 2 // 3
    half = width // 2
    main = jnp.where(side == 0, w_qkv[:, :width], w_qkv[:, half:])
    keys = even_rows(jnp.where(side == 0, w_qkv[:, width:], w_qkv[:, :half]))
    cut = keys.shape[0] // 2
    first, second = keys[:cut], keys[cut:]
    got = cross(jnp.where(side == 0, second, first))
    keys = jnp.concatenate([jnp.where(side == 0, first, got), jnp.where(side == 0, got, second)], axis=1)
    blocks = jnp.pad(jnp.concatenate([main, keys], axis=0), ((0, 0), (0, count * SLOT - width)))
    return blocks.reshape(rows + cut, count, SLOT).transpose(1, 0, 2)


def finish_heads(landed, other, side, rows, width):
    one, two = jnp.where(side == 0, landed, other), jnp.where(side == 0, other, landed)
    keys = jnp.concatenate([one[:, rows:], two[:, rows:]], axis=1)[:, :rows]
    heads = jnp.concatenate([one[:, :rows], keys, two[:, :rows]], axis=2)
    return heads.reshape(width, 3 * SLOT)


def return_heads(landed, side, count, rows, width):
    half = width // 2
    landed = landed.transpose(1, 0, 2).reshape(-1, count * SLOT)[:, :width]
    main, keys = landed[:rows], landed[rows:]
    low, high = keys[:, :half], keys[:, half:]
    got, own = cross(jnp.where(side == 0, high, low)), jnp.where(side == 0, low, high)
    keys = jnp.concatenate([jnp.where(side == 0, own, got), jnp.where(side == 0, got, own)], axis=0)[:rows]
    return jnp.where(
        side == 0, jnp.concatenate([main, keys], axis=1), jnp.concatenate([keys, main], axis=1)
    ).astype(F32)


def dot_nt(first, second):
    return lax.dot_general(first, second, (((1,), (1,)), ((), ())), preferred_element_type=F32)


def dot_nn(first, second):
    return lax.dot_general(first, second, (((1,), (0,)), ((), ())), preferred_element_type=F32)


def dot_tn(first, second):
    return lax.dot_general(first, second, (((0,), (0,)), ((), ())), preferred_element_type=F32)


VMEM_SPEC = pl.BlockSpec(memory_space=pltpu.VMEM)
SMEM_SPEC = pl.BlockSpec(memory_space=pltpu.SMEM)
ANY_SPEC = pl.BlockSpec(memory_space=pl.ANY)


def local_call(kernel, name, outs, ins, args, flops, scratch=(), exps=0):
    moved = sum(math.prod(x.shape) * x.dtype.itemsize for x in list(args) + list(outs))
    return pl.pallas_call(
        kernel,
        out_shape=tuple(outs),
        in_specs=list(ins),
        out_specs=tuple(VMEM_SPEC for _ in outs),
        scratch_shapes=list(scratch),
        compiler_params=pltpu.CompilerParams(vmem_limit_bytes=VMEM_LIMIT),
        cost_estimate=pl.CostEstimate(flops=flops, bytes_accessed=moved, transcendentals=exps),
        name=name,
    )(*args)


def shape_of(rows, cols, kind):
    return jax.ShapeDtypeStruct((rows, cols), kind)


def norm_blocks(blocks, gain, shift, width):
    count = len(blocks)

    def kernel(*refs):
        ins, gain_ref, shift_ref, outs = refs[:count], refs[count], refs[count + 1], refs[count + 2 :]
        for i in range(count):
            values = ins[i][...].astype(F32)
            lane = lax.broadcasted_iota(jnp.int32, (1, values.shape[1]), 1)
            centred = values - jnp.sum(values, axis=-1, keepdims=True) * (1.0 / width)
            centred = jnp.where(lane < width, centred, 0.0)
            spread_of = jnp.sum(centred * centred, axis=-1, keepdims=True) * (1.0 / width)
            normed = centred * lax.rsqrt(spread_of + EPSILON)
            outs[i][...] = (normed * gain_ref[...] + shift_ref[...]).astype(BF16)
            outs[count + i][...] = normed.astype(BF16)

    outs = [jax.ShapeDtypeStruct(x.shape, BF16) for x in blocks] * 2
    args = list(blocks) + [gain, shift]
    size = sum(x.size for x in blocks)
    result = local_call(kernel, "norm_blocks", outs, [VMEM_SPEC] * len(args), args, 10 * size)
    return list(result[:count]), list(result[count:])


def feed_blocks(blocks, cots, w_fc, w_proj, bias):
    count, (width, share) = len(blocks), w_fc.shape
    sizes = [x.shape[0] for x in blocks]
    rows = sum(sizes)

    def kernel(*refs):
        h_refs, c_refs = refs[:count], refs[count : 2 * count]
        fc_ref, proj_ref, bias_ref, act_ref, du_ref, sum_ref = refs[2 * count : 2 * count + 6]
        outs, results = refs[2 * count + 6 : 3 * count + 6], refs[3 * count + 6 :]
        rows_in = jnp.concatenate([ref[...] for ref in h_refs], axis=0)
        cot_in = jnp.concatenate([ref[...] for ref in c_refs], axis=0)
        act, slope = gelu_pair(dot_nn(rows_in, fc_ref[...]) + bias_ref[...])
        act_ref[...] = act.astype(BF16)
        grad = dot_nt(cot_in, proj_ref[...]) * slope
        sum_ref[...] = jnp.sum(grad, axis=0, keepdims=True)
        grad = grad.astype(BF16)
        du_ref[...] = grad
        terms = dot_nt(grad, fc_ref[...]).astype(BF16)
        output = dot_nn(act_ref[...], proj_ref[...]).astype(BF16)
        at = 0
        for i in range(count):
            outs[i][...] = terms[at : at + sizes[i]]
            results[i][...] = output[at : at + sizes[i]]
            at += sizes[i]

    outs = [shape_of(rows, share, BF16), shape_of(rows, share, BF16), shape_of(1, share, F32)]
    outs += [shape_of(size, width, BF16) for size in sizes] * 2
    args = list(blocks) + list(cots) + [w_fc, w_proj, bias]
    result = local_call(
        kernel, "feed_blocks", outs, [VMEM_SPEC] * len(args), args, 8 * rows * width * share, exps=rows * share
    )
    return result[0], result[1], result[2], list(result[3 : 3 + count]), list(result[3 + count :])


def input_blocks(grad, w_heads, normed):
    count, width = len(normed), w_heads.shape[0]
    sizes = [x.shape[0] for x in normed]

    def kernel(*refs):
        grad_ref, w_ref, n_refs, sum_ref, outs = refs[0], refs[1], refs[2 : 2 + count], refs[2 + count], refs[3 + count :]
        terms = dot_nt(grad_ref[...], w_ref[...])
        gains = jnp.zeros((1, width), F32)
        at = 0
        for i, size in enumerate(sizes):
            term = terms[at : at + size]
            at += size
            outs[i][...] = term.astype(BF16)
            gains += jnp.sum(term * n_refs[i][...].astype(F32), axis=0, keepdims=True)
        sum_ref[0:1, :] = gains
        sum_ref[1:2, :] = jnp.sum(terms, axis=0, keepdims=True)

    outs = [shape_of(2, width, F32)] + [shape_of(size, width, BF16) for size in sizes]
    args = [grad, w_heads] + list(normed)
    result = local_call(
        kernel, "input_blocks", outs, [VMEM_SPEC] * len(args), args, 2 * grad.size * width
    )
    return result[0], list(result[1:])


def weight_terms(flags, steps, grads, scale, count, rows, heads):
    flat = [block for blocks in steps for block in blocks]
    width, cols = flat[0].shape[1], grads[0].shape[1]
    cut = (rows + 1) // 2
    shape = (count, rows + cut, SLOT) if heads else (count, cut, cols)

    def kernel(*refs):
        flag_ref, h_refs = refs[0], refs[1 : 1 + len(flat)]
        g_refs, (keep_ref, send_ref, held, part) = refs[1 + len(flat) : -4], refs[-4:]
        product, index = None, 0
        for step, blocks in enumerate(steps):
            at = 0
            for block in blocks:
                size = block.shape[0]
                add = dot_tn(g_refs[step][at : at + size, :], h_refs[index][...])
                product = add if product is None else product + add
                at += size
                index += 1
        held[...] = product.T * scale

        def give(out_ref, second):
            for d in range(count):
                if heads:
                    lanes = slice(2 * SLOT, 3 * SLOT) if second else slice(0, SLOT)
                    part[0:rows, :] = held[d * rows : (d + 1) * rows, lanes]
                    first = d * rows + (cut if second else 0)
                    part[rows : rows + cut, :] = held[first : first + cut, SLOT : 2 * SLOT]
                    out_ref[d] = part[0 : rows + cut, :].astype(BF16)
                else:
                    first = d * rows + (cut if second else 0)
                    out_ref[d] = held[first : first + cut, :].astype(BF16)

        @pl.when(flag_ref[0] == 0)
        def _():
            give(keep_ref, False)
            give(send_ref, True)

        @pl.when(flag_ref[0] != 0)
        def _():
            give(keep_ref, True)
            give(send_ref, False)

    outs = [jax.ShapeDtypeStruct(shape, BF16)] * 2
    args = [flags] + flat + list(grads)
    ins = [SMEM_SPEC] + [VMEM_SPEC] * (len(args) - 1)
    scratch = [pltpu.VMEM((width, cols), F32), pltpu.VMEM((rows + cut + 8, SLOT), F32)]
    total_rows = sum(x.shape[0] for x in flat)
    return local_call(kernel, "weight_terms", outs, ins, args, 2 * total_rows * width * cols, scratch)


def proj_terms(acts, steps, scale):
    flat = [block for blocks in steps for block in blocks]
    width, share = flat[0].shape[1], acts[0].shape[1]

    def kernel(*refs):
        c_refs, a_refs, out_ref = refs[: len(flat)], refs[len(flat) : -1], refs[-1]
        product, index = None, 0
        for step, blocks in enumerate(steps):
            at = 0
            for block in blocks:
                size = block.shape[0]
                add = dot_tn(a_refs[step][at : at + size, :], c_refs[index][...])
                product = add if product is None else product + add
                at += size
                index += 1
        out_ref[...] = product * scale

    outs = [shape_of(share, width, F32)]
    args = flat + list(acts)
    total_rows = sum(x.shape[0] for x in flat)
    flops = 2 * total_rows * width * share
    return local_call(kernel, "proj_terms", outs, [VMEM_SPEC] * len(args), args, flops)[0]


def out_blocks(spot, mixed, grad, layout, size, scale):
    (rows, height), cols = mixed.shape, grad.shape[1]
    unit = height // (2 * size)
    plan = [entry for entries in layout for entry in entries]

    def kernel(spot_ref, o_ref, grad_ref, *refs):
        outs, held = refs[:-1], refs[-1]
        turned = o_ref[...].astype(F32).T.astype(BF16)
        held[...] = dot_nn(turned, grad_ref[...]) * scale
        for i, (offset, other) in enumerate(plan):
            device = device_at(size, spot_ref, offset, other)
            block = held[pl.ds(pl.multiple_of(device * unit, 8), outs[i].shape[0]), :]
            outs[i][...] = block.astype(BF16)

    outs = [shape_of(2 * unit if other is None else unit, cols, BF16) for _, other in plan]
    result = local_call(
        kernel,
        "out_blocks",
        outs,
        [SMEM_SPEC] + [VMEM_SPEC] * 2,
        [spot, mixed, grad],
        2 * rows * height * cols,
        [pltpu.VMEM((height, cols), F32)],
    )
    steps, at = [], 0
    for entries in layout:
        steps.append(list(result[at : at + len(entries)]))
        at += len(entries)
    return steps


def head_masks(scale):
    lane = lax.broadcasted_iota(jnp.int32, (1, SLOT), 1)
    return [jnp.where(lane < HEAD_DIM, scale, 0.0), jnp.where(lane < HEAD_DIM, 0.0, scale)]


def flipped(value):
    return value.astype(F32).T


def causal(tile):
    keys = lax.broadcasted_iota(jnp.int32, (tile, tile), 0)
    queries = lax.broadcasted_iota(jnp.int32, (tile, tile), 1)
    return keys <= queries


def span(index, size):
    return pl.ds(pl.multiple_of(index * size, size), size)


def tile_of(seq):
    return math.gcd(seq, 512)


def attend_forward(order, spot, blocks, w_heads, bias, layout, blk):
    size = len(layout) - 1
    chips = 2 * size
    seq = 4 * chips * blk
    width = w_heads.shape[0]
    tile = tile_of(seq)
    tiles = seq // tile
    flat = [(step, entry) for step, entries in enumerate(layout) for entry in entries]
    pieces = len(flat)

    def kernel(*refs):
        order_ref, spot_ref = refs[:2]
        h_refs = refs[2 : 2 + pieces]
        w_ref, bias_ref, o_ref, lse_ref, qs, ks, vs, held, vt, os, sems = refs[2 + pieces :]
        masks = head_masks(SCALE)
        copies, starts, at = [], [], 0
        for i in range(pieces):
            rows = h_refs[i].shape[0]
            copy = pltpu.make_async_copy(h_refs[i], held.at[pl.ds(at, rows), :], sems.at[i])
            copy.start()
            copies.append(copy)
            starts.append(at)
            at += rows

        index = 0
        for step, entries in enumerate(layout):
            first = starts[index]
            for i in range(len(entries)):
                copies[index + i].wait()
            rows = sum(h_refs[index + i].shape[0] for i in range(len(entries)))
            mixed = dot_nn(held[first : first + rows, :], w_ref[...]) + bias_ref[...]
            for i, (offset, other) in enumerate(entries):
                base = starts[index + i] - first
                device = device_at(chips, spot_ref, offset, other)
                for part in range(4 if other is None else 2):
                    there = span(order_ref[2 * device + part], blk)
                    block = mixed[base : base + blk].astype(BF16)
                    base += blk
                    query = block[:, :SLOT].astype(F32)
                    for head in range(2):
                        qs[head, there, :] = (query * masks[head]).astype(BF16)
                    ks[there, :] = block[:, SLOT : 2 * SLOT]
                    vs[there, :] = block[:, 2 * SLOT :]
            index += len(entries)

        def turn(t, carry):
            vt[t] = flipped(vs[span(t, tile), :]).astype(BF16)
            return carry

        lax.fori_loop(0, tiles, turn, 0)
        visible = causal(tile)

        def query_tile(i, carry):
            def key_tile(j, state, diagonal):
                fresh = []
                for head in range(2):
                    top, sums, accum = state[3 * head : 3 * head + 3]
                    scores = dot_nt(ks[span(j, tile), :], qs[head, span(i, tile), :])
                    if diagonal:
                        scores = jnp.where(visible, scores, NEG_LARGE)
                    new_top = jnp.maximum(top, jnp.max(scores, axis=0, keepdims=True))
                    terms = jnp.exp(scores - new_top)
                    decay = jnp.exp(top - new_top)
                    sums = sums * decay + jnp.sum(terms, axis=0, keepdims=True)
                    values = vt[j, head * HEAD_DIM : (head + 1) * HEAD_DIM, :]
                    accum = accum * decay + dot_nn(values, terms.astype(BF16))
                    fresh += [new_top, sums, accum]
                return tuple(fresh)

            start = (
                jnp.full((1, tile), NEG_LARGE, F32),
                jnp.zeros((1, tile), F32),
                jnp.zeros((HEAD_DIM, tile), F32),
            )
            state = lax.fori_loop(0, i, lambda j, state: key_tile(j, state, False), start + start)
            state = key_tile(i, state, True)
            mixed = jnp.concatenate([state[2] / state[1], state[5] / state[4]], axis=0)
            os[span(i, tile), :] = mixed.T.astype(BF16)
            for head in range(2):
                lse_ref[i, head : head + 1, :] = state[3 * head] + jnp.log(state[3 * head + 1])
            return carry

        lax.fori_loop(0, tiles, query_tile, 0)

        def sort_out(s, carry):
            o_ref[span(s, blk), :] = os[span(order_ref[s], blk), :]
            return carry

        lax.fori_loop(0, seq // blk, sort_out, 0)

    outs = [
        shape_of(seq, SLOT, BF16),
        jax.ShapeDtypeStruct((tiles, 8, tile), F32),
        jax.ShapeDtypeStruct((2, seq, SLOT), BF16),
        shape_of(seq, SLOT, BF16),
        shape_of(seq, SLOT, BF16),
    ]
    scratch = [
        pltpu.VMEM((seq, width), BF16),
        pltpu.VMEM((tiles, SLOT, tile), BF16),
        pltpu.VMEM((seq, SLOT), BF16),
        pltpu.SemaphoreType.DMA((pieces,)),
    ]
    args = [order, spot] + [block for step in blocks for block in step] + [w_heads, bias]
    ins = [SMEM_SPEC] * 2 + [ANY_SPEC] * pieces + [VMEM_SPEC] * 2
    flops = 4 * seq * seq * SLOT + 6 * seq * width * SLOT
    return local_call(kernel, "attend_forward", outs, ins, args, flops, scratch, seq * seq)


def attend_backward(order, spot, saved, grads, mixed, lse, layout, blk, w_heads=None, normed=None):
    queries, keys, values = saved
    seq = keys.shape[0]
    chips = 2 * (len(layout) - 1)
    tile = tile_of(seq)
    tiles = seq // tile
    steps = len(layout)
    flat = [block for blocks in normed for block in blocks] if normed else []
    pieces = len(flat)

    def kernel(order_ref, spot_ref, qs, ks, vs, g_ref, o_ref, lse_ref, *refs):
        if pieces:
            w_ref, n_refs, refs = refs[0], refs[1 : 1 + pieces], refs[1 + pieces :]
            norm_ref, t_refs = refs[1 + steps], refs[2 + steps : 2 + steps + pieces]
            held, sems = refs[-2:]
            copies, at = [], 0
            for i in range(pieces):
                rows = flat[i].shape[0]
                copy = pltpu.make_async_copy(n_refs[i], held.at[pl.ds(at, rows), :], sems.at[i])
                copy.start()
                copies.append(copy)
                at += rows
            refs = refs[: 1 + steps] + refs[2 + steps + pieces : -2]
        sum_ref, d_refs = refs[0], refs[1 : 1 + steps]
        gs, ps, kt, dqt, drow, dk, dv, dsort = refs[1 + steps :]
        g_masks = head_masks(1.0)

        def sort_in(s, carry):
            here, there = span(s, blk), span(order_ref[s], blk)
            g_block = g_ref[here, :].astype(F32)
            for head in range(2):
                gs[head, there, :] = (g_block * g_masks[head]).astype(BF16)
            ps[there, :] = g_block * o_ref[here, :].astype(F32)
            return carry

        lax.fori_loop(0, seq // blk, sort_in, 0)

        def turn(t, carry):
            kt[t] = flipped(ks[span(t, tile), :]).astype(BF16)
            products = ps[span(t, tile), :].T
            for head in range(2):
                drow[t, head : head + 1, :] = jnp.sum(
                    products[head * HEAD_DIM : (head + 1) * HEAD_DIM], axis=0, keepdims=True
                )
            dqt[t] = jnp.zeros((SLOT, tile), F32)
            return carry

        lax.fori_loop(0, tiles, turn, 0)
        visible = causal(tile)
        sum_ref[...] = jnp.zeros(sum_ref.shape, F32)

        def key_tile(j, carry):
            dk[...] = jnp.zeros(dk.shape, F32)
            dv[...] = jnp.zeros(dv.shape, F32)

            def query_tile(i, diagonal):
                key_add, value_add = [], []
                for head in range(2):
                    scores = dot_nt(ks[span(j, tile), :], qs[head, span(i, tile), :])
                    terms = jnp.exp(scores - lse_ref[i, head : head + 1, :])
                    if diagonal:
                        terms = jnp.where(visible, terms, 0.0)
                    slopes = dot_nt(vs[span(j, tile), :], gs[head, span(i, tile), :])
                    slopes = (terms * (slopes - drow[i, head : head + 1, :])).astype(BF16)
                    value_add.append(dot_nn(terms.astype(BF16), gs[head, span(i, tile), :]))
                    key_add.append(dot_nn(slopes, qs[head, span(i, tile), :]))
                    rows = slice(head * HEAD_DIM, (head + 1) * HEAD_DIM)
                    dqt[i, rows, :] += dot_nn(kt[j, rows, :], slopes)
                dk[...] += key_add[0] + key_add[1]
                dv[...] += value_add[0] + value_add[1]

            query_tile(j, True)

            def later(i, carry):
                query_tile(i, False)
                return carry

            lax.fori_loop(j + 1, tiles, later, 0)
            dsort[1, span(j, tile), :] = dk[...].astype(BF16)
            dsort[2, span(j, tile), :] = dv[...].astype(BF16)
            sum_ref[1:2, :] += jnp.sum(dv[...], axis=0, keepdims=True)
            return carry

        lax.fori_loop(0, tiles, key_tile, 0)

        def finish(t, carry):
            query_grad = dqt[t].T * SCALE
            dsort[0, span(t, tile), :] = query_grad.astype(BF16)
            sum_ref[0:1, :] += jnp.sum(query_grad, axis=0, keepdims=True)
            return carry

        lax.fori_loop(0, tiles, finish, 0)

        for step, entries in enumerate(layout):
            base = 0
            for offset, other in entries:
                device = device_at(chips, spot_ref, offset, other)
                for part in range(4 if other is None else 2):
                    there = span(order_ref[2 * device + part], blk)
                    for kind in range(3):
                        d_refs[step][base : base + blk, kind * SLOT : (kind + 1) * SLOT] = dsort[kind, there, :]
                    base += blk

        if pieces:
            for copy in copies:
                copy.wait()
            gains, shifts, at, index = 0.0, 0.0, 0, 0
            for step, blocks in enumerate(normed):
                terms = dot_nt(d_refs[step][...], w_ref[...])
                shifts = shifts + jnp.sum(terms, axis=0, keepdims=True)
                first = 0
                for block in blocks:
                    rows = block.shape[0]
                    term = terms[first : first + rows]
                    t_refs[index][...] = term.astype(BF16)
                    values = held[at : at + rows, :].astype(F32)
                    gains = gains + jnp.sum(term * values, axis=0, keepdims=True)
                    first, at, index = first + rows, at + rows, index + 1
            norm_ref[0:1, :] = gains
            norm_ref[1:2, :] = shifts

    outs = [shape_of(8, SLOT, F32)]
    for entries in layout:
        rows = sum(4 * blk if other is None else 2 * blk for _, other in entries)
        outs.append(shape_of(rows, 3 * SLOT, BF16))
    scratch = [
        pltpu.VMEM((2, seq, SLOT), BF16),
        pltpu.VMEM((seq, SLOT), F32),
        pltpu.VMEM((tiles, SLOT, tile), BF16),
        pltpu.VMEM((tiles, SLOT, tile), F32),
        pltpu.VMEM((tiles, 8, tile), F32),
        pltpu.VMEM((tile, SLOT), F32),
        pltpu.VMEM((tile, SLOT), F32),
        pltpu.VMEM((3, seq, SLOT), BF16),
    ]
    args = [order, spot, queries, keys, values, grads, mixed, lse]
    ins = [SMEM_SPEC] * 2 + [VMEM_SPEC] * 6
    flops = 10 * seq * seq * SLOT
    if pieces:
        width = w_heads.shape[0]
        args += [w_heads] + flat
        ins += [VMEM_SPEC] + [ANY_SPEC] * pieces
        outs += [shape_of(2, width, F32)] + [shape_of(block.shape[0], width, BF16) for block in flat]
        scratch += [pltpu.VMEM((seq, width), BF16), pltpu.SemaphoreType.DMA((pieces,))]
        flops += 6 * seq * width * SLOT
    result = local_call(kernel, "attend_backward", outs, ins, args, flops, scratch, seq * seq)
    terms, at = [], 2 + steps
    for blocks in normed or []:
        terms.append(list(result[at : at + len(blocks)]))
        at += len(blocks)
    return list(result[1 : 1 + steps]), result[0], terms, result[1 + steps] if pieces else None


def body(
    tokens,
    cotangent,
    block_order,
    ln1_gain,
    ln1_bias,
    w_qkv,
    qv_bias,
    w_out,
    out_bias,
    ln2_gain,
    ln2_bias,
    w_fc,
    fc_bias,
    w_proj,
    proj_bias,
):
    width = HEADS * HEAD_DIM
    half = width // 2
    count = lax.axis_size("context")
    rows = tokens.shape[1]
    seq = count * rows
    blk = rows // 2
    hidden = fc_bias.shape[0] * 2
    share = hidden // count
    own_rows = w_qkv.shape[0]
    padded = count * SLOT
    grad_scale = 1.0 / math.sqrt(lax.axis_size("fsdp") * seq)
    side = lax.axis_index("fsdp")
    ring = Ring(count)
    mine, layout, far = ring.mine, ring.layout(), ring.far
    upper = mine // (count // 2)
    order = block_order.astype(jnp.int32)
    spot = ring.spot
    sizes = [[2 * rows if other is None else rows for _, other in entries] for entries in layout]

    vectors = jnp.concatenate(
        [
            jnp.stack(
                [ln1_gain, ln1_bias, qv_bias[:, 0], qv_bias[:, 1], out_bias, ln2_gain, ln2_bias, proj_bias]
            ),
            fc_bias.reshape(-1, half),
        ],
        axis=0,
    )
    low, high = pair_halves(vectors, side)
    rows_of = jnp.concatenate([low[:8], high[:8]], axis=1).astype(F32)
    gain_one, shift_one, q_bias, v_bias, out_b, gain_two, shift_two, proj_b = [rows_of[i : i + 1] for i in range(8)]
    fc_b = jnp.concatenate([low[8:].reshape(-1), high[8:].reshape(-1)])
    fc_b = lax.dynamic_slice(fc_b, (mine * share,), (share,)).astype(F32)[None]
    slot_bias = jnp.concatenate([q_bias, jnp.zeros_like(q_bias), v_bias], axis=0)
    slot_bias = jnp.pad(slot_bias, ((0, 0), (0, padded - width)))
    slot_bias = lax.dynamic_slice(slot_bias, (0, mine * SLOT), (3, SLOT)).reshape(1, 3 * SLOT)

    xs16 = tokens[0]
    xs = xs16.astype(F32)
    head_blocks = start_heads(w_qkv, side, count)
    landed_heads = spread(head_blocks)
    other_heads = cross(landed_heads)
    w_heads = wide(finish_heads(landed_heads, other_heads, side, own_rows, width), 0)
    x_steps, h_one, n_one = [], [], []

    def visit_tokens(step, blocks):
        h_blocks, n_blocks = norm_blocks(blocks, wide(gain_one), wide(shift_one), width)
        x_steps.append(blocks)
        h_one.append(h_blocks)
        n_one.append(n_blocks)
        return h_blocks[0]

    cot16 = cotangent[0]
    cot_wide = wide(cot16)

    low, high = pair_halves(w_out, side)
    w_out_rows = jnp.concatenate([low, high], axis=1)
    w_out_rows = jnp.pad(w_out_rows, ((0, -own_rows % 8), (0, 0)))
    out_rows = w_out_rows.shape[0]
    fc_blocks = start_fc(w_fc, side, count, share)
    made = {}

    def hold_tokens(step, value):
        if step == 1:
            value = after(value, w_out_rows)
        if step == 2:
            value = after(value, head_blocks)
        if step == 3:
            value = after(value, landed_heads)
        if step == far:
            value = after(value, fc_blocks, other_heads)
        made["tokens"] = value
        return value

    ring.gather(wide(xs16), visit_tokens, hold_tokens)

    w_out_all = lax.all_gather(after(w_out_rows, made["tokens"]), "context", axis=0, tiled=True)
    landed_fc = spread(after(fc_blocks, x_steps[far - 1][0]))
    low, high = pair_halves(after(w_proj, w_heads), side)
    w_proj_part = wide(jnp.concatenate([low, high], axis=1))

    mixed, lse, *saved = attend_forward(order, spot, h_one, w_heads, slot_bias, layout, blk)

    cot_steps = []
    ring.gather(
        cot_wide,
        lambda step, blocks: cot_steps.append(blocks),
        lambda step, value: after(value, made["tokens"] if step == 1 else mixed) if step <= 2 else value,
    )

    w_fc_part = wide(finish_fc(after(landed_fc, mixed), side, upper, own_rows), 0)
    mixed = after(mixed, landed_fc, w_proj_part, cot_steps[max(1, far // 4)][0])
    attn_out = lax.all_to_all(mixed, "context", 0, 1, tiled=True)[:, :width]
    attn_out = after(attn_out, w_fc_part, cot_steps[max(2, 3 * far // 4)][0]).reshape(rows, count, own_rows)
    attn_out = jnp.pad(attn_out, ((0, 0), (0, 0), (0, out_rows - own_rows))).reshape(rows, -1)

    resid_one = xs + dot_nn(attn_out, w_out_all) + out_b
    normed_two, inv_two = norm_stats(resid_one)
    h_two = (normed_two * gain_two + shift_two).astype(BF16)

    h_steps, acts, slopes, bias_sums, h2_terms, out_terms = [], [], [], [], [], []

    def visit_feed(step, blocks):
        act, slope, bias_sum, terms, outputs = feed_blocks(
            blocks, cot_steps[step], w_fc_part, w_proj_part, fc_b
        )
        h_steps.append(blocks)
        acts.append(act)
        slopes.append(slope)
        bias_sums.append(bias_sum)
        h2_terms.append(terms)
        out_terms.append(outputs)
        return bias_sum

    ring.gather(wide(h_two), visit_feed)

    is_first = (upper == side).astype(jnp.int32)

    def fill_feed(step, event):
        if step == far:
            flags = after(1 - is_first, event).reshape(1)
            made["fc"] = weight_terms(flags, h_steps, slopes, grad_scale, count, own_rows, False)
            made["fc_got"] = cross(made["fc"][1])
            return (made["fc"][1],)
        if step == far - 1:
            made["proj"] = proj_terms([after(acts[0], event)] + acts[1:], cot_steps, grad_scale)
            return (made["proj"],)
        if step == far - 2:
            g_proj = after(made["proj"], event)[:, :width]
            left, right = g_proj[:, :half], g_proj[:, half:]
            made["proj_keep"] = jnp.where(side == 0, left, right)
            send = jnp.where(side == 0, right, left).astype(BF16)
            made["proj_got"] = cross(send)
            made["fc_sum"] = total([after(made["fc"][0], event), made["fc_got"]]).astype(BF16)
            return (send, made["fc_sum"])
        return ()

    grad_h2 = ring.scatter(lambda step, event: h2_terms[step], fill_feed)[:, :width]

    grad_y = cot16.astype(F32)
    normed_one, inv_one = norm_stats(xs)
    grad_r1 = grad_y + norm_back(grad_h2, normed_two, inv_two, gain_two)
    grad_r16 = grad_r1.astype(BF16)
    grad_o16 = dot_nt(grad_r16, w_out_all).astype(BF16)
    grad_o16 = grad_o16.reshape(rows, count, out_rows)[:, :, :own_rows].reshape(rows, width)
    grad_slots = jnp.pad(grad_o16, ((0, 0), (0, padded - width)))
    grad_heads = lax.all_to_all(grad_slots, "context", 1, 0, tiled=True)

    g_out_steps = out_blocks(spot, after(attn_out, grad_slots), wide(grad_r16), layout, ring.size, grad_scale)
    out_grad_ring = Scatter(ring, lambda step, event: g_out_steps[step])
    out_grad_ring.hop()

    out_ring = Scatter(ring, lambda step, event: out_terms[step])
    out_ring.hop(grad_o16)
    out_ring.hop()

    fc_sum = made["fc_sum"]
    fc_landed = spread(after(fc_sum, grad_heads))
    grad_heads = after(grad_heads, out_ring.sent, out_grad_ring.sent, made["proj_got"])
    fused = seq * width <= 4 * 1024 * 1024
    d_steps, head_sums, h1_terms, h1_sums = attend_backward(
        order, spot, saved, grad_heads, mixed, lse, layout, blk, *((w_heads, n_one) if fused else ())
    )
    norm_sums = [h1_sums] if fused else []

    def give_input(step, event):
        if fused:
            return h1_terms[step]
        event = made[2] if step == 0 else event
        grad = d_steps[step] if event is None else after(d_steps[step], event)
        sums, terms = input_blocks(grad, w_heads, n_one[step])
        norm_sums.append(sums)
        return terms

    input_ring = Scatter(ring, give_input)
    input_ring.hop(out_ring.got, out_grad_ring.got, fc_landed)
    made[far] = input_ring.sent
    out_ring.hop(input_ring.sent)
    out_grad_ring.hop(input_ring.sent)
    input_ring.hold(out_ring.sent, out_grad_ring.sent)
    for step in range(far - 1, 1, -1):
        input_ring.hop()
        made[step] = event = input_ring.sent
        if step == far - 1:
            flags = after(side, event).astype(jnp.int32).reshape(1)
            keep, send = weight_terms(flags, h_one, d_steps, grad_scale, count, own_rows, True)
            got = cross(send)
            out_ring.hop(event)
            input_ring.hold(send, out_ring.sent)
        if step == far - 2:
            out_grad_ring.hop(event)
            input_ring.hold(out_grad_ring.sent)
    input_ring.hop()
    made[1] = input_ring.sent
    qkv_sum = total([after(keep, made[1]), got]).astype(BF16)
    out_grad_ring.hop(made[1])
    grad_h1 = input_ring.finish()[:, :width]
    grad_x = (grad_r1 + norm_back(grad_h1, normed_one, inv_one, gain_one)).astype(BF16)
    result = (resid_one + out_ring.finish()[:, :width] + proj_b).astype(BF16)
    g_out = out_grad_ring.finish()[:own_rows]
    g_w_out = pair_sum(g_out[:, :half], g_out[:, half:width], side)
    g_w_qkv = return_heads(spread(qkv_sum), side, count, own_rows, width)
    g_w_proj = total([after(made["proj_keep"], made[1]), made["proj_got"]])
    g_w_fc = return_fc(after(fc_landed, qkv_sum), side, count, own_rows)

    fc_place = lax.dynamic_update_slice(jnp.zeros((hidden,), F32), total(bias_sums)[0], (mine * share,))
    head_place = lax.dynamic_update_slice(
        jnp.zeros((2, padded), F32), head_sums[:2], (jnp.int32(0), mine * SLOT)
    )[:, :width]
    local = jnp.concatenate(
        [
            jnp.sum(grad_h2 * normed_two, axis=0),
            jnp.sum(grad_h2, axis=0),
            jnp.sum(grad_r1, axis=0),
            jnp.sum(grad_y, axis=0),
            fc_place,
            total(norm_sums)[:, :width].reshape(-1),
            head_place.reshape(-1),
        ]
    )
    sums = sum_everywhere(after(local, out_grad_ring.sent).reshape(-1, SLOT) * grad_scale, count).reshape(-1)

    def own_half(vector):
        return lax.dynamic_slice(vector, (side * (vector.shape[0] // 2),), (vector.shape[0] // 2,))

    g_ln2_gain, g_ln2_bias, g_out_bias, g_proj_bias = [
        own_half(sums[i * width : (i + 1) * width]) for i in range(4)
    ]
    g_fc_bias = own_half(sums[4 * width : 4 * width + hidden])
    late = sums[4 * width + hidden :]
    g_ln1_gain, g_ln1_bias, g_q, g_v = [own_half(late[i * width : (i + 1) * width]) for i in range(4)]
    return (
        result[None],
        grad_x[None],
        g_ln1_gain,
        g_ln1_bias,
        g_w_qkv,
        jnp.stack([g_q, g_v], axis=1),
        g_w_out,
        g_out_bias,
        g_ln2_gain,
        g_ln2_bias,
        g_w_fc,
        g_fc_bias,
        g_w_proj,
        g_proj_bias,
    )


def solution(mesh):
    rows = P("fsdp", "context", None)
    weight = P("context", "fsdp")
    vector = P("fsdp")
    pair = P("fsdp", None)
    return jax.shard_map(
        body,
        mesh=mesh,
        in_specs=(
            rows, rows, P(), vector, vector, weight, pair, weight,
            vector, vector, vector, weight, vector, weight, vector,
        ),
        out_specs=(
            rows, rows, vector, vector, weight, pair, weight,
            vector, vector, vector, weight, vector, weight, vector,
        ),
        check_vma=False,
    )
```
